32 devices in a mesh: row: 8 (over z, y), col: 4 (over x, core).
Axes of the slice: x: 2, y: 2, z: 4, core: 2. Of those that a mesh axis runs over, the one named last changes fastest.
Arguments:
- factor: bfloat16 [8192, 8192], P('row', 'col'), may hold values from -0.078125 to 0.078125
- diag_inv: bfloat16 [8192, 1024], P('row'), may hold values from -1 to 1.5, as said below
- rhs: bfloat16 [8192, 256], P('row'), may hold values from -6 to 6
- forward_values: bfloat16 [8192, 256], P('row'), may hold values from -6 to 6
Outputs:
- forward_solved: bfloat16 [3072, 256], replicated
- forward_rest: float32 [8192, 256], P('row', 'col')
- back_sums: float32 [8192, 256], P('col', 'row')
- solution: float32 [8192, 256], P('row')
The draws below stay inside these ranges and needn't reach their ends.
Inputs may be any that keep to these rules, and one draw needn't show every extreme that they name: Each 1024 x 1024 block of diag_inv is lower triangular with diagonal entries between 0.5 and 1.5.
All inputs are finite; a program needn't handle non-finite values.
Results may differ from the reference program's by a relative error of at most 0.0095.
Values may be sent and summed in bfloat16 or wider, within the bound.
No kernel may reach another device: no remote copies, remote signals or barrier semaphores. Data moves between devices by JAX's collectives and lax.ppermute only.
A program may use at most 64 MiB of HBM per device.

```python
import math
import jax
import jax.numpy as jnp
from jax import lax

NB = 1024
R = 256
STEPS = 3
NBLK = 8
N = 8192
N_ROW = 8
N_COL = 4


def draw_diag_inv(key, part):
    key = jax.random.fold_in(key, 7)
    first_key, second_key = jax.random.split(key)
    shape = (NBLK, NB, NB)
    row_pos = lax.broadcasted_iota(jnp.int32, shape, 1)
    col_pos = lax.broadcasted_iota(jnp.int32, shape, 2)
    scale = 1.0 / math.sqrt(NB)
    diagonal = jax.random.uniform(first_key, shape, jnp.float32, 0.7, 1.3)
    lower = jax.random.normal(second_key, shape, jnp.float32) * (0.6 * scale)
    full = jnp.where(row_pos == col_pos, diagonal, jnp.where(row_pos > col_pos, lower, 0.0))
    return full.reshape(NBLK * NB, NB).astype(jnp.bfloat16)


def steps_of(stream_key, extent, shards, low, largest):
    factor_of, own = 1.0, jax.random.fold_in(stream_key, 6)
    for dim, shards_of in shards:
        steps = jnp.exp(jax.random.uniform(jax.random.fold_in(own, dim), (shards_of,), jnp.float32, low / len(shards), largest / len(shards)))
        factor_of = factor_of * jnp.repeat(steps, extent[dim] // shards_of).reshape([-1 if axis == dim else 1 for axis in range(len(extent))])
    return factor_of


def scatter_about(rng, dims, scale, most, cuts=(), held_as=jnp.bfloat16):
    values = jax.random.normal(rng, dims, jnp.float32) * scale
    if len(cuts) > 0:
        values = steps_of(rng, dims, cuts, -0.22, 0.18) * values
    return jnp.clip(values, min=-most, max=most).astype(held_as)


def setup_inputs(seed: int = 0) -> dict:
    key_of = jax.random.split(jax.random.key(seed), 5)
    return {
        "factor": scatter_about(key_of[0], (N, N), (2 * NB * STEPS) ** -0.5, 0.078125, ((0, 8), (1, 4))),
        "diag_inv": draw_diag_inv(jax.random.fold_in(key_of[4], 71), 0),
        "rhs": scatter_about(key_of[2], (N, R), 1.0, 6.0, ((0, 8),)),
        "forward_values": scatter_about(key_of[3], (N, R), 1.0, 6.0, ((0, 8),)),
    }


def block_at(factor, row_index, col_index):
    return factor[row_index * NB:(row_index + 1) * NB, col_index * NB:(col_index + 1) * NB]


def reference(factor, diag_inv, rhs, forward_values):
    row_blocks = NBLK // N_ROW
    col_blocks = NBLK // N_COL
    forward_blocks = []
    rest_blocks = []
    for position in range(NBLK):
        summed = jnp.zeros((NB, R), jnp.float32)
        for group in range(N_COL):
            group_sum = jnp.zeros((NB, R), jnp.float32)
            for other in range(group * col_blocks, (group + 1) * col_blocks):
                if other < min(position, STEPS):
                    group_sum = group_sum + jnp.dot(block_at(factor, position, other), forward_blocks[other], preferred_element_type=jnp.float32)
            summed = summed + lax.optimization_barrier(group_sum.astype(jnp.bfloat16)).astype(jnp.float32)
        rest = rhs[position * NB:(position + 1) * NB].astype(jnp.float32) - summed
        rest_blocks.append(rest)
        if position < STEPS:
            residue = rest.astype(jnp.bfloat16)
            inverse = diag_inv[position * NB:(position + 1) * NB]
            forward_blocks.append(jnp.dot(inverse, residue, preferred_element_type=jnp.float32).astype(jnp.bfloat16))
    first_back = NBLK - STEPS
    answers = [None] * NBLK
    rounded_answers = [None] * NBLK
    sum_blocks = [None] * NBLK
    for position in reversed(range(NBLK)):
        summed = jnp.zeros((NB, R), jnp.float32)
        for group in range(N_ROW):
            group_sum = jnp.zeros((NB, R), jnp.float32)
            for other in range(group * row_blocks, (group + 1) * row_blocks):
                if other > position and other >= first_back:
                    group_sum = group_sum + jnp.dot(block_at(factor, other, position).T, rounded_answers[other], preferred_element_type=jnp.float32)
            summed = summed + lax.optimization_barrier(group_sum.astype(jnp.bfloat16)).astype(jnp.float32)
        sum_blocks[position] = summed
        if position >= first_back:
            gathered_sum = summed.astype(jnp.bfloat16)
            earlier = forward_values[position * NB:(position + 1) * NB]
            centred = (earlier.astype(jnp.float32) - gathered_sum.astype(jnp.float32)).astype(jnp.bfloat16)
            inverse = diag_inv[position * NB:(position + 1) * NB]
            answers[position] = jnp.dot(inverse.T, centred, preferred_element_type=jnp.float32)
            rounded_answers[position] = answers[position].astype(jnp.bfloat16)
        else:
            answers[position] = jnp.zeros((NB, R), jnp.float32)
    return (jnp.concatenate(forward_blocks, axis=0), jnp.concatenate(rest_blocks, axis=0), jnp.concatenate(sum_blocks, axis=0), jnp.concatenate(answers, axis=0))
```

```python
import functools

import jax
import jax.numpy as jnp
from jax import lax
from jax.experimental import pallas as pl
from jax.experimental.pallas import tpu as pltpu
from jax.sharding import PartitionSpec as P

NB = 1024
STEPS = 3
BOTH = ("row", "col")
BF16, F32 = jnp.bfloat16, jnp.float32


def nn(a, b):
    return jnp.dot(a, b, preferred_element_type=F32)


def nt(a, b):
    return lax.dot_general(a, b, (((1,), (1,)), ((), ())), preferred_element_type=F32)


def flip(x):
    return jnp.transpose(x.astype(F32))


class Copies:
    def __init__(self, sems):
        self.sems = sems
        self.used = 0

    def branch(self):
        self.used = 0

    def start(self, src, dst):
        copy = pltpu.make_async_copy(src, dst, self.sems.at[self.used])
        copy.start()
        self.used += 1
        return copy


def call(kernel, ins, outs, scratch, sems, aliases=None, limit=16, order=()):
    any_space = pl.BlockSpec(memory_space=pl.ANY)
    used, ins = len(ins), list(ins) + list(order)
    outs = list(outs) + [((8, 128), F32)]

    def body(*refs):
        n = len(ins) + len(outs)
        kernel(*refs[:used], *refs[len(ins) : n - 1], *refs[n:])

    return pl.pallas_call(
        body,
        out_shape=[jax.ShapeDtypeStruct(s, d) for s, d in outs],
        in_specs=[any_space] * len(ins),
        out_specs=[any_space] * len(outs),
        scratch_shapes=[pltpu.VMEM(s, d) for s, d in scratch] + [pltpu.SemaphoreType.DMA((sems,))],
        input_output_aliases=aliases or {},
        compiler_params=pltpu.CompilerParams(vmem_limit_bytes=limit << 20),
        cost_estimate=pl.CostEstimate(flops=0, bytes_accessed=0, transcendentals=0),
    )(*ins)


def local(factor, diag_inv, rhs, forward_values):
    rows = lax.axis_size("row")
    cols = lax.axis_size("col")
    cb = factor.shape[1] // NB
    wide = rhs.shape[1]
    assert factor.shape[0] == NB and rows % 4 == 0 and cols % 2 == 0 and rows >= 8 and cb <= 2
    share = wide // cols
    row_share = wide // rows
    piece = cb * row_share
    last = rows - 1
    pairs = rows // 2
    all_cols = range(cols)
    evens = range(0, cols, 2)
    group = lambda j: j // cb
    g0, g1, g2, g5, g6 = group(0), group(1), group(2), group(last - 2), group(last - 1)
    evens5 = [d for d in evens if d // 2 != g5 // 2]
    full, square, tall = (wide, NB), (NB, NB), (NB, wide)
    pair_piece = (2, piece, NB)

    def place():
        return lax.axis_index("row"), lax.axis_index("col")

    def send(x, pairs):
        return lax.ppermute(x, BOTH, [(a * cols + b, d * cols + e) for (a, b), (d, e) in pairs])

    def block(ref, j):
        return ref.at[:, pl.ds((j % cb) * NB, NB)]

    def multiply(q_ref, v, fac, limit):
        _, c = place()
        for b in range(cb):
            q = nn(v, fac[b])
            q = jnp.where(c * cb + b < limit, q, 0.0).astype(BF16)
            q_ref[:, :, b * row_share : (b + 1) * row_share, :] = q.reshape(pairs, 2, row_share, NB)

    def rolled(cp, buf, outs):
        _, c = place()
        return [
            cp.start(buf.at[pl.ds(pl.multiple_of(lax.rem(c + s, cols) * share, share), share)], outs[s])
            for s in all_cols
        ]

    def wait(copies):
        for o in copies:
            o.wait()

    def route(cases, shape, order=(), through=(), times=1):
        n, m = len(cases), len(through)

        def kernel(*refs):
            outs, buf, sems = refs[n + m : n + m + times], refs[-2], refs[-1]
            r, c = place()
            cp = Copies(sems)
            for (cond, _), ref in zip(cases, refs):
                cp.branch()

                @pl.when(cond(r, c))
                def _(ref=ref):
                    cp.start(ref, buf).wait()
                    wait([cp.start(buf, out) for out in outs])

        return call(
            kernel,
            [v for _, v in cases] + list(through),
            [(shape, BF16)] * times + [(x.shape, x.dtype) for x in through],
            [(shape, BF16)],
            1 + times,
            aliases={n + k: times + k for k in range(m)},
            order=order,
        )

    def at(row, col):
        return lambda r, c: (r == row) & (c == col)

    def kernel0(fac, inv, rh, fv, x_out, v_out, y_out, dbuf, lbuf, rbuf, xbuf, vbuf, sems):
        r, c = place()
        cp = Copies(sems)

        @pl.when(r == 0)
        def _():
            ins = [cp.start(rh, rbuf), cp.start(inv, dbuf)]
            ins[0].wait()
            z = flip(rbuf[...]).astype(BF16)
            ins[1].wait()
            xbuf[...] = nt(z, dbuf[...]).astype(BF16)
            own = xbuf.at[pl.ds(pl.multiple_of(c * share, share), share)]
            wait([cp.start(xbuf, x_out), cp.start(own, y_out)])

        cp.branch()

        @pl.when(r == last)
        def _():
            ins = [cp.start(fv, rbuf), cp.start(inv, dbuf)]
            for g, j in ((g6, last - 1), (g5, last - 2)):

                @pl.when(c == g)
                def _(j=j):
                    pltpu.make_async_copy(block(fac, j), lbuf, sems.at[4]).start()

            ins[0].wait()
            w = flip(rbuf[...]).astype(BF16)
            ins[1].wait()
            vbuf[...] = nn(w, dbuf[...])
            v = cp.start(vbuf, v_out)

            @pl.when((c == g6) | (c == g5))
            def _():
                pltpu.make_async_copy(block(fac, 0), lbuf, sems.at[4]).wait()
                xbuf[...] = nn(vbuf[...].astype(BF16), lbuf[...]).astype(BF16)
                cp.start(xbuf, x_out).wait()

            v.wait()

    x1, v7, y0_own, _ = call(
        kernel0,
        [factor, diag_inv, rhs, forward_values],
        [(full, BF16), (full, F32), ((share, NB), BF16)],
        [(square, BF16), (square, BF16), (tall, BF16), (full, BF16), (full, F32)],
        5,
        limit=60,
    )
    q_more = [send(x1, [((last, g6), (last - 1, d)), ((last, g5), (last - 2, d))]) for d in evens5[1:]]
    a1 = send(x1, [((0, g0), (1, g0)), ((last, g6), (last - 1, g5)), ((last, g5), (last - 2, evens5[0]))])
    a2 = send(x1, [((0, g0), (2, g0)), ((last, g6), (last - 1, evens5[0])), ((last, g5), (last - 2, g5))])
    t6_parts = [a2] + q_more
    q75_parts = [a1] + q_more
    entry = [0, 3] + [2 * d for d in range(2, pairs)]
    y0_z = {e: send(y0_own, [((0, b), (e, b)) for b in all_cols]) for e in entry[1:]}

    def kernel7(v_in, fac, *rest):
        sol_out, bq, (fbuf, vbuf, qbuf, sbuf, zbuf, sems) = rest[0], rest[1 : 1 + pairs], rest[1 + pairs :]
        r, _ = place()
        cp = Copies(sems)

        @pl.when(r == last)
        def _():
            fs = [cp.start(fac.at[:, pl.ds(k * NB, NB)], fbuf.at[k]) for k in range(cb)]
            cp.start(v_in, vbuf).wait()
            wait(fs)
            v = vbuf[...]
            multiply(qbuf, v.astype(BF16), fbuf, last)
            done = [cp.start(qbuf.at[d], bq[d]) for d in range(pairs)]
            sbuf[...] = jnp.transpose(v)
            wait(done + [cp.start(sbuf, sol_out)])

        cp.branch()

        @pl.when(r < last - 2)
        def _():
            zbuf[...] = jnp.zeros_like(zbuf)
            wait([cp.start(zbuf, sol_out.at[pl.ds(k * wide, wide)]) for k in range(NB // wide)])

    sol, *bq, tok = call(
        kernel7,
        [v7, factor],
        [(tall, F32)] + [(pair_piece, BF16)] * pairs,
        [((cb, NB, NB), BF16), (full, F32), ((pairs, 2, piece, NB), BF16), (tall, F32), ((wide, wide), F32)],
        2 + cb + pairs,
    )

    y0_cases = [(lambda r, c: r == 0, y0_own)] + [(lambda r, c, e=e: r == e, v) for e, v in y0_z.items()]
    y0_in, tok = route(y0_cases, (share, NB), order=[tok])
    y0_out = send(y0_in, [((e, b), (e ^ 1, b)) for e in entry for b in all_cols])

    def kernel1(p1, fac, inv, rh, fv, x_out, *rest):
        outs, (dbuf, lbuf, rbuf, abuf, xbuf, sems) = rest[:cols], rest[cols:]
        r, c = place()
        cp = Copies(sems)

        @pl.when((r == 1) & (c == g0))
        def _():
            ins = [cp.start(rh, rbuf), cp.start(p1, abuf), cp.start(block(fac, 0), lbuf), cp.start(inv, dbuf)]
            ins[0].wait()
            z = flip(rbuf[...])
            ins[1].wait()
            ins[2].wait()
            z = z - nt(abuf[...], lbuf[...]).astype(BF16).astype(F32)
            ins[3].wait()
            xbuf[...] = nt(z.astype(BF16), dbuf[...]).astype(BF16)
            wait([cp.start(xbuf, x_out)] + rolled(cp, xbuf, outs))

        cp.branch()

        @pl.when((r == last - 1) & (c == g5))
        def _():
            ins = [cp.start(fv, rbuf), cp.start(p1, abuf), cp.start(inv, dbuf), cp.start(block(fac, last - 2), lbuf)]
            ins[0].wait()
            w = flip(rbuf[...])
            ins[1].wait()
            w = w - abuf[...].astype(F32)
            ins[2].wait()
            v = nn(w.astype(BF16), dbuf[...]).astype(BF16)
            ins[3].wait()
            xbuf[...] = nn(v, lbuf[...]).astype(BF16)
            cp.start(xbuf, x_out).wait()

    x3, *parts, tok = call(
        kernel1,
        [a1, factor, diag_inv, rhs, forward_values],
        [(full, BF16)] + [((share, NB), BF16)] * cols,
        [(square, BF16), (square, BF16), (tall, BF16), (full, BF16), (full, BF16)],
        5 + cols,
        order=[tok],
    )
    a3 = send(x3, [((1, g0), (2, g1)), ((last - 1, g5), (last - 2, g5))])
    a4 = [send(x3, [((last - 1, g5), (last - 2, d))]) for d in evens5]

    def within_chip(row, owner):
        own = [((row, owner), (row, owner ^ 1))]
        return own + [((row, d), (row, d + 1)) for d in evens if d // 2 != owner // 2]

    def kernels0(p1, p2, fac, *rest):
        more, (out, lbuf, abuf, xbuf, sems) = rest[: len(evens5) - 1], rest[len(evens5) - 1 :]
        r, c = place()
        cp = Copies(sems)

        @pl.when((r == 2) & (c == g0))
        def _():
            wait([cp.start(p2, abuf), cp.start(block(fac, 0), lbuf)])
            xbuf[...] = nt(abuf[...], lbuf[...]).astype(BF16)
            cp.start(xbuf, out).wait()

        for col, ref in zip([g5] + evens5, [p1, p2] + list(more)):
            cp.branch()

            @pl.when((r == last - 1) & (c == col))
            def _(ref=ref):
                cp.start(ref, xbuf).wait()
                cp.start(xbuf, out).wait()

    t6_even, tok = call(
        kernels0,
        [a1, a2, factor] + q_more,
        [(full, BF16)],
        [(square, BF16), (full, BF16), (full, BF16)],
        3,
        order=[tok],
    )
    s0 = t6_even if g0 == g1 else send(t6_even, [((2, g0), (2, g1))])

    t6_odd = send(t6_even, within_chip(last - 1, g5))

    def is_entry(r, c):
        return ((r % 2 == 0) & (r != 2)) | (r == 3)

    y0_mine, tok = route(
        [(is_entry, y0_in), (lambda r, c: jnp.logical_not(is_entry(r, c)), y0_out)], (share, NB), [tok]
    )

    def kernel2(p0, p1, fac, inv, rh, *rest):
        outs, (dbuf, lbuf, rbuf, abuf, bbuf, xbuf, sems) = rest[cols : 2 * cols], rest[2 * cols :]
        r, c = place()
        cp = Copies(sems)

        @pl.when((r == 2) & (c == g1))
        def _():
            ins = [cp.start(rh, rbuf), cp.start(p1, abuf), cp.start(block(fac, 1), lbuf), cp.start(p0, bbuf), cp.start(inv, dbuf)]
            ins[0].wait()
            z = flip(rbuf[...])
            wait(ins[1:4])
            s = nt(abuf[...], lbuf[...]) + bbuf[...].astype(F32)
            z = z - s.astype(BF16).astype(F32)
            ins[4].wait()
            xbuf[...] = nt(z.astype(BF16), dbuf[...]).astype(BF16)
            wait(rolled(cp, xbuf, outs))

    *parts, tok = call(
        kernel2,
        [s0, a3, factor, diag_inv, rhs] + parts,
        [((share, NB), BF16)] * cols,
        [(square, BF16), (square, BF16), (tall, BF16), (full, BF16), (full, BF16), (full, BF16)],
        5 + cols,
        aliases={5 + k: k for k in range(cols)},
        order=[tok],
    )
    dealt = [send(parts[s], [((1, g0), (1, (g0 + s) % cols)), ((2, g1), (2, (g1 + s) % cols))]) for s in range(1, cols)]

    cases = [(at(1, g0), parts[0]), (at(2, g1), parts[0])]
    for s in range(1, cols):
        cases += [(at(1, (g0 + s) % cols), dealt[s - 1]), (at(2, (g1 + s) % cols), dealt[s - 1])]
    y_own, tok = route(cases, (share, NB), order=[tok])
    to_odd = [pairs - 1] + [d for d in range(1, pairs - 1)]
    to_even = [pairs - 1, 0] + [d for d in range(2, pairs - 1)]
    y_z = [
        send(y_own, [((1, b), (2 * d + 1, b)) for b in all_cols] + [((2, b), (2 * e, b)) for b in all_cols])
        for d, e in zip(to_odd, to_even)
    ]

    def kernelt(*refs):
        n = len(evens5) + 1
        first, second, (_, out, _, abuf, bbuf, sems) = refs[:n], refs[n : 2 * n], refs[2 * n :]
        r, c = place()
        cp = Copies(sems)
        for col, x, q in zip([g5] + evens5, first, second):
            cp.branch()

            @pl.when((r == last - 2) & (c == col))
            def _(x=x, q=q):
                wait([cp.start(x, abuf), cp.start(q, bbuf)])
                abuf[...] = (abuf[...].astype(F32) + bbuf[...].astype(F32)).astype(BF16)
                cp.start(abuf, out).wait()

    t5_even, y0_mine, tok = call(
        kernelt,
        [a3] + a4 + [a2] + q75_parts + [y0_mine],
        [(full, BF16), ((share, NB), BF16)],
        [(full, BF16), (full, BF16)],
        3,
        aliases={2 * len(evens5) + 2: 1},
        order=[tok],
    )
    t5_odd = send(t5_even, within_chip(last - 2, g5))

    y0_all = lax.all_gather(y0_mine, "col", axis=0, tiled=True)
    cases = [(lambda r, c: (r == 1) | (r == 2), y_own)]
    for d, e, v in zip(to_odd, to_even, y_z):
        cases.append((lambda r, c, d=d, e=e: (r == 2 * d + 1) | (r == 2 * e), v))
    y_mine, y_near, tok = route(cases, (share, NB), order=[tok, y0_all], times=2)
    all_swap = [((a, b), (a ^ 1, b)) for a in range(rows) for b in all_cols]
    y_other = send(y_mine, all_swap)

    i = last - 2
    slots = {d: d + 1 for d in range(pairs - 2)}
    slots.update({pairs - 1: 0, pairs - 2: pairs - 1})
    own_slots = {d: d for d in range(pairs)}

    def lands(d):
        return 2 * d if d < (pairs - 2) // 2 else 2 * d + 1

    def kernel5(t6e, t6o, t5e, t5o, fac, inv, fv, *rest):
        n = pairs + 2
        sol_out, outs = rest[n], rest[n + 1 : n + 1 + pairs]
        dbuf, fbuf, rbuf, abuf, qbuf, sbuf, sems = rest[2 * n :]
        r, c = place()
        cp = Copies(sems)
        has = (c == g5) | ((c % 2 == 0) & (c // 2 != g5 // 2))
        sem = sems.at[3 + cb + pairs]

        for row, te, to, to_slot in ((last - 1, t6e, t6o, own_slots), (i, t5e, t5o, slots)):
            cp.branch()

            @pl.when(r == row)
            def _(row=row, te=te, to=to, to_slot=to_slot):
                ins = [cp.start(fv, rbuf), cp.start(inv, dbuf)]
                fs = [cp.start(fac.at[:, pl.ds(k * NB, NB)], fbuf.at[k]) for k in range(cb)]

                @pl.when(has)
                def _():
                    pltpu.make_async_copy(te, abuf, sem).start()

                @pl.when(jnp.logical_not(has))
                def _():
                    pltpu.make_async_copy(to, abuf, sem).start()

                ins[0].wait()
                w = flip(rbuf[...])
                pltpu.make_async_copy(te, abuf, sem).wait()
                w = w - abuf[...].astype(F32)
                ins[1].wait()
                v = nn(w.astype(BF16), dbuf[...])
                wait(fs)
                multiply(qbuf, v.astype(BF16), fbuf, row)
                done = [cp.start(qbuf.at[d], outs[t]) for d, t in to_slot.items()]
                sbuf[...] = jnp.transpose(v)
                wait(done + [cp.start(sbuf, sol_out)])

    sol, *bq, y_near, tok = call(
        kernel5,
        [t6_even, t6_odd, t5_even, t5_odd, factor, diag_inv, forward_values, sol] + bq + [y_near],
        [(tall, F32)] + [(pair_piece, BF16)] * pairs + [((share, NB), BF16)],
        [(square, BF16), ((cb, NB, NB), BF16), (tall, BF16), (full, BF16), ((pairs, 2, piece, NB), BF16), (tall, F32)],
        4 + cb + pairs,
        aliases={7 + k: k for k in range(pairs + 2)},
        order=[tok],
    )
    scattered = []
    for t in range(pairs - 1):
        to = [d for d, k in slots.items() if k == t][0]
        pairs_t = [((last, b), (2 * t + 1, b)) for b in all_cols] + [((last - 1, b), (2 * t, b)) for b in all_cols]
        scattered.append(send(bq[t], pairs_t + [((i, b), (lands(to), b)) for b in all_cols]))

    near_all = lax.all_gather(y_near, "col", axis=0, tiled=True)

    far_all = lax.all_gather(y_other, "col", axis=0, tiled=True)

    def load_by_parity(even, odd, buf, sem):
        r, _ = place()
        for parity, ref in enumerate((even, odd)):

            @pl.when(lax.rem(r, 2) == parity)
            def _(ref=ref):
                pltpu.make_async_copy(ref, buf, sem).start()

        return pltpu.make_async_copy(even, buf, sem)

    def kernelb(own_q, *rest):
        got, (own_out, part_out, bbuf, fbuf, obuf, pbuf, sems) = rest[: pairs - 1], rest[pairs - 1 :]
        r, _ = place()
        cp = Copies(sems)
        pair = r // 2
        refs = list(got) + [own_q]
        for d in range(pairs):
            cp.branch()

            @pl.when(pair == d)
            def _(d=d):
                cp.start(refs[d], bbuf).wait()

            @pl.when(r == lands(d))
            def _(d=d):
                cp.start(refs[slots[d]], fbuf).wait()

        cp.branch()

        takes = functools.reduce(jnp.logical_or, [r == lands(d) for d in range(pairs)])
        for y in (0, 1):
            for more in (False, True):

                @pl.when((lax.rem(r, 2) == y) & (takes if more else jnp.logical_not(takes)))
                def _(y=y, more=more):
                    ours, theirs = bbuf[y].astype(F32), bbuf[1 - y].astype(F32)
                    if more:
                        ours = ours + fbuf[y].astype(F32)
                        theirs = theirs + fbuf[1 - y].astype(F32)
                    obuf[...] = ours
                    pbuf[...] = theirs.astype(BF16)

        wait([cp.start(pbuf, part_out), cp.start(obuf, own_out)])

    own, part, tok = call(
        kernelb,
        [bq[pairs - 1]] + scattered,
        [((piece, NB), F32), ((piece, NB), BF16)],
        [(pair_piece, BF16), (pair_piece, BF16), ((piece, NB), F32), ((piece, NB), BF16)],
        2,
        order=[tok, near_all, far_all],
    )
    theirs = send(part, all_swap)

    owners = sorted({g0, g1, g2})

    def kernelr(y0, near, far, fac, *rest):
        outs, (lbuf, abuf, pbuf, sems) = rest[:cols], rest[cols:]
        r, c = place()
        cp = Copies(sems)

        for g in owners:
            cp.branch()

            @pl.when(c == g)
            def _(g=g):
                ins = []
                if g == g0:
                    ins.append((0, cp.start(y0, abuf.at[0]), cp.start(block(fac, 0), lbuf.at[0])))
                for k, gk, even, odd in ((1, g1, far, near), (2, g2, near, far)):
                    if gk == g:
                        n = len(ins)
                        a = load_by_parity(even, odd, abuf.at[n], sems.at[4 + cols])
                        ins.append((k, a, cp.start(block(fac, k), lbuf.at[n])))
                total = None
                for n, (k, a, b) in enumerate(ins):
                    a.wait()
                    b.wait()
                    p = jnp.where(r > k, nt(abuf[n], lbuf[n]), 0.0)
                    total = p if total is None else total + p
                pbuf[...] = total.astype(BF16)
                wait(rolled(cp, pbuf, outs))

    *p_parts, tok = call(
        kernelr,
        [y0_all, near_all, far_all, factor],
        [((share, NB), BF16)] * cols,
        [((2, NB, NB), BF16), ((2,) + full, BF16), (full, BF16)],
        5 + cols,
        order=[tok],
    )
    p_got = [
        send(p_parts[s], [((a, g), (a, (g + s) % cols)) for a in range(1, rows) for g in owners]) for s in range(1, cols)
    ]

    def kernelo(y0, near, far, rh, own_p, fs_out, side_out, abuf, tbuf, rbuf, pbuf, obuf, sems):
        _, c = place()
        cp = Copies(sems)
        ins = [cp.start(y0, abuf.at[0])]
        ins.append(load_by_parity(far, near, abuf.at[1], sems.at[7]))
        ins.append(load_by_parity(near, far, abuf.at[2], sems.at[8]))
        more = [cp.start(rh, rbuf), cp.start(own_p, pbuf)]
        done = []
        for k in range(STEPS):
            ins[k].wait()
            tbuf[k] = flip(abuf[k]).astype(BF16)
            done.append(cp.start(tbuf.at[k], fs_out.at[pl.ds(k * NB, NB)]))
        wait(more)
        side = flip(rbuf[...])
        for d in all_cols:

            @pl.when(c == d)
            def _(d=d):
                base = side[d * share : (d + 1) * share]
                obuf[...] = base - pbuf[...].astype(F32) if d in owners else base

        wait(done + [cp.start(obuf, side_out)])

    solved, side, tok = call(
        kernelo,
        [y0_all, near_all, far_all, rhs, p_parts[0]],
        [((STEPS * NB, wide), BF16), ((share, NB), F32)],
        [((STEPS,) + full, BF16), ((STEPS,) + tall, BF16), (tall, BF16), ((share, NB), BF16), ((share, NB), F32)],
        9,
        order=[tok],
    )

    rest = side - sum(x.astype(F32) for x in p_got)
    total = own + theirs.astype(F32)
    sums = jnp.concatenate([total[b * row_share : (b + 1) * row_share] for b in range(cb)], axis=1)
    return (solved, jnp.transpose(rest), jnp.transpose(sums), sol)


def solution(mesh):
    placed = (P("row", "col"), P("row", None), P("row", None), P("row", None))
    return jax.shard_map(
        local,
        mesh=mesh,
        in_specs=placed,
        out_specs=(P(), P("row", "col"), P("col", "row"), P("row", None)),
        check_vma=False,
    )
```

```python
import functools

import jax
import jax.numpy as jnp
from jax import lax
from jax.experimental import pallas as pl
from jax.experimental.pallas import tpu as pltpu
from jax.sharding import PartitionSpec as P

NB = 1024
STEPS = 3
BOTH = ("row", "col")
BF16, F32 = jnp.bfloat16, jnp.float32


def nn(a, b):
    return jnp.dot(a, b, preferred_element_type=F32)


def nt(a, b):
    return lax.dot_general(a, b, (((1,), (1,)), ((), ())), preferred_element_type=F32)


def flip(x):
    return jnp.transpose(x.astype(F32))


class Copies:
    def __init__(self, sems):
        self.sems = sems
        self.used = 0

    def branch(self):
        self.used = 0

    def start(self, src, dst):
        copy = pltpu.make_async_copy(src, dst, self.sems.at[self.used])
        copy.start()
        self.used += 1
        return copy


def call(kernel, ins, outs, scratch, sems, aliases=None, limit=16, order=()):
    any_space = pl.BlockSpec(memory_space=pl.ANY)
    used, ins = len(ins), list(ins) + list(order)
    outs = list(outs) + [((8, 128), F32)]

    def body(*refs):
        n = len(ins) + len(outs)
        kernel(*refs[:used], *refs[len(ins) : n - 1], *refs[n:])

    return pl.pallas_call(
        body,
        out_shape=[jax.ShapeDtypeStruct(s, d) for s, d in outs],
        in_specs=[any_space] * len(ins),
        out_specs=[any_space] * len(outs),
        scratch_shapes=[pltpu.VMEM(s, d) for s, d in scratch] + [pltpu.SemaphoreType.DMA((sems,))],
        input_output_aliases=aliases or {},
        compiler_params=pltpu.CompilerParams(vmem_limit_bytes=limit << 20),
        cost_estimate=pl.CostEstimate(flops=0, bytes_accessed=0, transcendentals=0),
    )(*ins)


def local(factor, diag_inv, rhs, forward_values):
    rows = lax.axis_size("row")
    cols = lax.axis_size("col")
    cb = factor.shape[1] // NB
    wide = rhs.shape[1]
    assert factor.shape[0] == NB and rows % 4 == 0 and cols % 2 == 0 and rows >= 8 and cb <= 2
    share = wide // cols
    row_share = wide // rows
    piece = cb * row_share
    last = rows - 1
    pairs = rows // 2
    all_cols = range(cols)
    evens = range(0, cols, 2)
    group = lambda j: j // cb
    g0, g1, g2, g5, g6 = group(0), group(1), group(2), group(last - 2), group(last - 1)
    evens5 = [d for d in evens if d // 2 != g5 // 2]
    full, square, tall = (wide, NB), (NB, NB), (NB, wide)
    pair_piece = (2, piece, NB)

    def place():
        return lax.axis_index("row"), lax.axis_index("col")

    def send(x, pairs):
        return lax.ppermute(x, BOTH, [(a * cols + b, d * cols + e) for (a, b), (d, e) in pairs])

    def block(ref, j):
        return ref.at[:, pl.ds((j % cb) * NB, NB)]

    def multiply(q_ref, v, fac, limit):
        _, c = place()
        for b in range(cb):
            q = nn(v, fac[b])
            q = jnp.where(c * cb + b < limit, q, 0.0).astype(BF16)
            q_ref[:, :, b * row_share : (b + 1) * row_share, :] = q.reshape(pairs, 2, row_share, NB)

    def rolled(cp, buf, outs):
        _, c = place()
        return [
            cp.start(buf.at[pl.ds(pl.multiple_of(lax.rem(c + s, cols) * share, share), share)], outs[s])
            for s in all_cols
        ]

    def wait(copies):
        for o in copies:
            o.wait()

    def route(cases, shape, order=(), through=(), times=1):
        n, m = len(cases), len(through)

        def kernel(*refs):
            outs, buf, sems = refs[n + m : n + m + times], refs[-2], refs[-1]
            r, c = place()
            cp = Copies(sems)
            for (cond, _), ref in zip(cases, refs):
                cp.branch()

                @pl.when(cond(r, c))
                def _(ref=ref):
                    cp.start(ref, buf).wait()
                    wait([cp.start(buf, out) for out in outs])

        return call(
            kernel,
            [v for _, v in cases] + list(through),
            [(shape, BF16)] * times + [(x.shape, x.dtype) for x in through],
            [(shape, BF16)],
            1 + times,
            aliases={n + k: times + k for k in range(m)},
            order=order,
        )

    def at(row, col):
        return lambda r, c: (r == row) & (c == col)

    def kernel0(fac, inv, rh, fv, x_out, v_out, y_out, dbuf, lbuf, rbuf, xbuf, vbuf, sems):
        r, c = place()
        cp = Copies(sems)

        @pl.when(r == 0)
        def _():
            ins = [cp.start(rh, rbuf), cp.start(inv, dbuf)]
            ins[0].wait()
            z = flip(rbuf[...]).astype(BF16)
            ins[1].wait()
            xbuf[...] = nt(z, dbuf[...]).astype(BF16)
            own = xbuf.at[pl.ds(pl.multiple_of(c * share, share), share)]
            wait([cp.start(xbuf, x_out), cp.start(own, y_out)])

        cp.branch()

        @pl.when(r == last)
        def _():
            ins = [cp.start(fv, rbuf), cp.start(inv, dbuf)]
            for g, j in ((g6, last - 1), (g5, last - 2)):

                @pl.when(c == g)
                def _(j=j):
                    pltpu.make_async_copy(block(fac, j), lbuf, sems.at[4]).start()

            ins[0].wait()
            w = flip(rbuf[...]).astype(BF16)
            ins[1].wait()
            vbuf[...] = nn(w, dbuf[...])
            v = cp.start(vbuf, v_out)

            @pl.when((c == g6) | (c == g5))
            def _():
                pltpu.make_async_copy(block(fac, 0), lbuf, sems.at[4]).wait()
                xbuf[...] = nn(vbuf[...].astype(BF16), lbuf[...]).astype(BF16)
                cp.start(xbuf, x_out).wait()

            v.wait()

    x1, v7, y0_own, _ = call(
        kernel0,
        [factor, diag_inv, rhs, forward_values],
        [(full, BF16), (full, F32), ((share, NB), BF16)],
        [(square, BF16), (square, BF16), (tall, BF16), (full, BF16), (full, F32)],
        5,
        limit=60,
    )
    q_more = [send(x1, [((last, g6), (last - 1, d)), ((last, g5), (last - 2, d))]) for d in evens5[1:]]
    a1 = send(x1, [((0, g0), (1, g0)), ((last, g6), (last - 1, g5)), ((last, g5), (last - 2, evens5[0]))])
    a2 = send(x1, [((0, g0), (2, g0)), ((last, g6), (last - 1, evens5[0])), ((last, g5), (last - 2, g5))])
    t6_parts = [a2] + q_more
    q75_parts = [a1] + q_more
    entry = [0, 3] + [2 * d for d in range(2, pairs)]
    y0_z = {e: send(y0_own, [((0, b), (e, b)) for b in all_cols]) for e in entry[1:]}

    def kernel7(v_in, fac, *rest):
        sol_out, bq, (fbuf, vbuf, qbuf, sbuf, zbuf, sems) = rest[0], rest[1 : 1 + pairs], rest[1 + pairs :]
        r, _ = place()
        cp = Copies(sems)

        @pl.when(r == last)
        def _():
            fs = [cp.start(fac.at[:, pl.ds(k * NB, NB)], fbuf.at[k]) for k in range(cb)]
            cp.start(v_in, vbuf).wait()
            wait(fs)
            v = vbuf[...]
            multiply(qbuf, v.astype(BF16), fbuf, last)
            done = [cp.start(qbuf.at[d], bq[d]) for d in range(pairs)]
            sbuf[...] = jnp.transpose(v)
            wait(done + [cp.start(sbuf, sol_out)])

        cp.branch()

        @pl.when(r < last - 2)
        def _():
            zbuf[...] = jnp.zeros_like(zbuf)
            wait([cp.start(zbuf, sol_out.at[pl.ds(k * wide, wide)]) for k in range(NB // wide)])

    sol, *bq, tok = call(
        kernel7,
        [v7, factor],
        [(tall, F32)] + [(pair_piece, BF16)] * pairs,
        [((cb, NB, NB), BF16), (full, F32), ((pairs, 2, piece, NB), BF16), (tall, F32), ((wide, wide), F32)],
        2 + cb + pairs,
    )

    y0_cases = [(lambda r, c: r == 0, y0_own)] + [(lambda r, c, e=e: r == e, v) for e, v in y0_z.items()]
    y0_in, tok = route(y0_cases, (share, NB), order=[tok])
    y0_out = send(y0_in, [((e, b), (e ^ 1, b)) for e in entry for b in all_cols])

    def kernel1(p1, fac, inv, rh, fv, x_out, *rest):
        outs, (dbuf, lbuf, rbuf, abuf, xbuf, sems) = rest[:cols], rest[cols:]
        r, c = place()
        cp = Copies(sems)

        @pl.when((r == 1) & (c == g0))
        def _():
            ins = [cp.start(rh, rbuf), cp.start(p1, abuf), cp.start(block(fac, 0), lbuf), cp.start(inv, dbuf)]
            ins[0].wait()
            z = flip(rbuf[...])
            ins[1].wait()
            ins[2].wait()
            z = z - nt(abuf[...], lbuf[...]).astype(BF16).astype(F32)
            ins[3].wait()
            xbuf[...] = nt(z.astype(BF16), dbuf[...]).astype(BF16)
            wait([cp.start(xbuf, x_out)] + rolled(cp, xbuf, outs))

        cp.branch()

        @pl.when((r == last - 1) & (c == g5))
        def _():
            ins = [cp.start(fv, rbuf), cp.start(p1, abuf), cp.start(inv, dbuf), cp.start(block(fac, last - 2), lbuf)]
            ins[0].wait()
            w = flip(rbuf[...])
            ins[1].wait()
            w = w - abuf[...].astype(F32)
            ins[2].wait()
            v = nn(w.astype(BF16), dbuf[...]).astype(BF16)
            ins[3].wait()
            xbuf[...] = nn(v, lbuf[...]).astype(BF16)
            cp.start(xbuf, x_out).wait()

    x3, *parts, tok = call(
        kernel1,
        [a1, factor, diag_inv, rhs, forward_values],
        [(full, BF16)] + [((share, NB), BF16)] * cols,
        [(square, BF16), (square, BF16), (tall, BF16), (full, BF16), (full, BF16)],
        5 + cols,
        order=[tok],
    )
    a3 = send(x3, [((1, g0), (2, g1)), ((last - 1, g5), (last - 2, g5))])
    a4 = [send(x3, [((last - 1, g5), (last - 2, d))]) for d in evens5]

    def within_chip(row, owner):
        own = [((row, owner), (row, owner ^ 1))]
        return own + [((row, d), (row, d + 1)) for d in evens if d // 2 != owner // 2]

    def kernels0(p1, p2, fac, *rest):
        more, (out, lbuf, abuf, xbuf, sems) = rest[: len(evens5) - 1], rest[len(evens5) - 1 :]
        r, c = place()
        cp = Copies(sems)

        @pl.when((r == 2) & (c == g0))
        def _():
            wait([cp.start(p2, abuf), cp.start(block(fac, 0), lbuf)])
            xbuf[...] = nt(abuf[...], lbuf[...]).astype(BF16)
            cp.start(xbuf, out).wait()

        for col, ref in zip([g5] + evens5, [p1, p2] + list(more)):
            cp.branch()

            @pl.when((r == last - 1) & (c == col))
            def _(ref=ref):
                cp.start(ref, xbuf).wait()
                cp.start(xbuf, out).wait()

    t6_even, tok = call(
        kernels0,
        [a1, a2, factor] + q_more,
        [(full, BF16)],
        [(square, BF16), (full, BF16), (full, BF16)],
        3,
        order=[tok],
    )
    s0 = t6_even if g0 == g1 else send(t6_even, [((2, g0), (2, g1))])

    t6_odd = send(t6_even, within_chip(last - 1, g5))

    def kernel2(p0, p1, fac, inv, rh, *rest):
        outs, (dbuf, lbuf, rbuf, abuf, bbuf, xbuf, sems) = rest[cols : 2 * cols], rest[2 * cols :]
        r, c = place()
        cp = Copies(sems)

        @pl.when((r == 2) & (c == g1))
        def _():
            ins = [cp.start(rh, rbuf), cp.start(p1, abuf), cp.start(block(fac, 1), lbuf), cp.start(p0, bbuf), cp.start(inv, dbuf)]
            ins[0].wait()
            z = flip(rbuf[...])
            wait(ins[1:4])
            s = nt(abuf[...], lbuf[...]) + bbuf[...].astype(F32)
            z = z - s.astype(BF16).astype(F32)
            ins[4].wait()
            xbuf[...] = nt(z.astype(BF16), dbuf[...]).astype(BF16)
            wait(rolled(cp, xbuf, outs))

    *parts, tok = call(
        kernel2,
        [s0, a3, factor, diag_inv, rhs] + parts,
        [((share, NB), BF16)] * cols,
        [(square, BF16), (square, BF16), (tall, BF16), (full, BF16), (full, BF16), (full, BF16)],
        5 + cols,
        aliases={5 + k: k for k in range(cols)},
        order=[tok],
    )
    dealt = [send(parts[s], [((1, g0), (1, (g0 + s) % cols)), ((2, g1), (2, (g1 + s) % cols))]) for s in range(1, cols)]

    def is_entry(r, c):
        return ((r % 2 == 0) & (r != 2)) | (r == 3)

    y0_mine, tok = route(
        [(is_entry, y0_in), (lambda r, c: jnp.logical_not(is_entry(r, c)), y0_out)], (share, NB), [tok]
    )

    cases = [(at(1, g0), parts[0]), (at(2, g1), parts[0])]
    for s in range(1, cols):
        cases += [(at(1, (g0 + s) % cols), dealt[s - 1]), (at(2, (g1 + s) % cols), dealt[s - 1])]
    y_own, y0_mine, tok = route(cases, (share, NB), order=[tok], through=[y0_mine])
    to_odd = [pairs - 1] + [d for d in range(1, pairs - 1)]
    to_even = [pairs - 1, 0] + [d for d in range(2, pairs - 1)]
    y_z = [
        send(y_own, [((1, b), (2 * d + 1, b)) for b in all_cols] + [((2, b), (2 * e, b)) for b in all_cols])
        for d, e in zip(to_odd, to_even)
    ]

    y0_all = lax.all_gather(y0_mine, "col", axis=0, tiled=True)
    cases = [(lambda r, c: (r == 1) | (r == 2), y_own)]
    for d, e, v in zip(to_odd, to_even, y_z):
        cases.append((lambda r, c, d=d, e=e: (r == 2 * d + 1) | (r == 2 * e), v))
    y_mine, y_near, tok = route(cases, (share, NB), order=[tok, y0_all], times=2)
    all_swap = [((a, b), (a ^ 1, b)) for a in range(rows) for b in all_cols]
    y_other = send(y_mine, all_swap)

    def kernelt(*refs):
        n = len(evens5) + 1
        first, second, (_, out, _, abuf, bbuf, sems) = refs[:n], refs[n : 2 * n], refs[2 * n :]
        r, c = place()
        cp = Copies(sems)
        for col, x, q in zip([g5] + evens5, first, second):
            cp.branch()

            @pl.when((r == last - 2) & (c == col))
            def _(x=x, q=q):
                wait([cp.start(x, abuf), cp.start(q, bbuf)])
                abuf[...] = (abuf[...].astype(F32) + bbuf[...].astype(F32)).astype(BF16)
                cp.start(abuf, out).wait()

    t5_even, y_near, tok = call(
        kernelt,
        [a3] + a4 + [a2] + q75_parts + [y_near],
        [(full, BF16), ((share, NB), BF16)],
        [(full, BF16), (full, BF16)],
        3,
        aliases={2 * len(evens5) + 2: 1},
        order=[tok],
    )
    t5_odd = send(t5_even, within_chip(last - 2, g5))

    near_all = lax.all_gather(y_near, "col", axis=0, tiled=True)

    i = last - 2
    slots = {d: d + 1 for d in range(pairs - 2)}
    slots.update({pairs - 1: 0, pairs - 2: pairs - 1})
    own_slots = {d: d for d in range(pairs)}

    def lands(d):
        return 2 * d if d < (pairs - 2) // 2 else 2 * d + 1

    def kernel5(t6e, t6o, t5e, t5o, fac, inv, fv, *rest):
        n = pairs + 2
        sol_out, outs = rest[n], rest[n + 1 : n + 1 + pairs]
        dbuf, fbuf, rbuf, abuf, qbuf, sbuf, sems = rest[2 * n :]
        r, c = place()
        cp = Copies(sems)
        has = (c == g5) | ((c % 2 == 0) & (c // 2 != g5 // 2))
        sem = sems.at[3 + cb + pairs]

        for row, te, to, to_slot in ((last - 1, t6e, t6o, own_slots), (i, t5e, t5o, slots)):
            cp.branch()

            @pl.when(r == row)
            def _(row=row, te=te, to=to, to_slot=to_slot):
                ins = [cp.start(fv, rbuf), cp.start(inv, dbuf)]
                fs = [cp.start(fac.at[:, pl.ds(k * NB, NB)], fbuf.at[k]) for k in range(cb)]

                @pl.when(has)
                def _():
                    pltpu.make_async_copy(te, abuf, sem).start()

                @pl.when(jnp.logical_not(has))
                def _():
                    pltpu.make_async_copy(to, abuf, sem).start()

                ins[0].wait()
                w = flip(rbuf[...])
                pltpu.make_async_copy(te, abuf, sem).wait()
                w = w - abuf[...].astype(F32)
                ins[1].wait()
                v = nn(w.astype(BF16), dbuf[...])
                wait(fs)
                multiply(qbuf, v.astype(BF16), fbuf, row)
                done = [cp.start(qbuf.at[d], outs[t]) for d, t in to_slot.items()]
                sbuf[...] = jnp.transpose(v)
                wait(done + [cp.start(sbuf, sol_out)])

    sol, *bq, y_other, tok = call(
        kernel5,
        [t6_even, t6_odd, t5_even, t5_odd, factor, diag_inv, forward_values, sol] + bq + [y_other],
        [(tall, F32)] + [(pair_piece, BF16)] * pairs + [((share, NB), BF16)],
        [(square, BF16), ((cb, NB, NB), BF16), (tall, BF16), (full, BF16), ((pairs, 2, piece, NB), BF16), (tall, F32)],
        4 + cb + pairs,
        aliases={7 + k: k for k in range(pairs + 2)},
        order=[tok, near_all],
    )
    scattered = []
    for t in range(pairs - 1):
        to = [d for d, k in slots.items() if k == t][0]
        pairs_t = [((last, b), (2 * t + 1, b)) for b in all_cols] + [((last - 1, b), (2 * t, b)) for b in all_cols]
        scattered.append(send(bq[t], pairs_t + [((i, b), (lands(to), b)) for b in all_cols]))

    far_all = lax.all_gather(y_other, "col", axis=0, tiled=True)

    def load_by_parity(even, odd, buf, sem):
        r, _ = place()
        for parity, ref in enumerate((even, odd)):

            @pl.when(lax.rem(r, 2) == parity)
            def _(ref=ref):
                pltpu.make_async_copy(ref, buf, sem).start()

        return pltpu.make_async_copy(even, buf, sem)

    owners = sorted({g0, g1, g2})

    def kernelr(y0, near, far, fac, *rest):
        outs, (lbuf, abuf, pbuf, sems) = rest[:cols], rest[cols:]
        r, c = place()
        cp = Copies(sems)

        for g in owners:
            cp.branch()

            @pl.when(c == g)
            def _(g=g):
                ins = []
                if g == g0:
                    ins.append((0, cp.start(y0, abuf.at[0]), cp.start(block(fac, 0), lbuf.at[0])))
                for k, gk, even, odd in ((1, g1, far, near), (2, g2, near, far)):
                    if gk == g:
                        n = len(ins)
                        a = load_by_parity(even, odd, abuf.at[n], sems.at[4 + cols])
                        ins.append((k, a, cp.start(block(fac, k), lbuf.at[n])))
                total = None
                for n, (k, a, b) in enumerate(ins):
                    a.wait()
                    b.wait()
                    p = jnp.where(r > k, nt(abuf[n], lbuf[n]), 0.0)
                    total = p if total is None else total + p
                pbuf[...] = total.astype(BF16)
                wait(rolled(cp, pbuf, outs))

    *p_parts, tok = call(
        kernelr,
        [y0_all, near_all, far_all, factor],
        [((share, NB), BF16)] * cols,
        [((2, NB, NB), BF16), ((2,) + full, BF16), (full, BF16)],
        5 + cols,
        order=[tok],
    )
    p_got = [
        send(p_parts[s], [((a, g), (a, (g + s) % cols)) for a in range(1, rows) for g in owners]) for s in range(1, cols)
    ]

    def kernelb(own_q, *rest):
        got, (own_out, part_out, bbuf, fbuf, obuf, pbuf, sems) = rest[: pairs - 1], rest[pairs - 1 :]
        r, _ = place()
        cp = Copies(sems)
        pair = r // 2
        refs = list(got) + [own_q]
        for d in range(pairs):
            cp.branch()

            @pl.when(pair == d)
            def _(d=d):
                cp.start(refs[d], bbuf).wait()

            @pl.when(r == lands(d))
            def _(d=d):
                cp.start(refs[slots[d]], fbuf).wait()

        cp.branch()

        takes = functools.reduce(jnp.logical_or, [r == lands(d) for d in range(pairs)])
        for y in (0, 1):
            for more in (False, True):

                @pl.when((lax.rem(r, 2) == y) & (takes if more else jnp.logical_not(takes)))
                def _(y=y, more=more):
                    ours, theirs = bbuf[y].astype(F32), bbuf[1 - y].astype(F32)
                    if more:
                        ours = ours + fbuf[y].astype(F32)
                        theirs = theirs + fbuf[1 - y].astype(F32)
                    obuf[...] = ours
                    pbuf[...] = theirs.astype(BF16)

        wait([cp.start(pbuf, part_out), cp.start(obuf, own_out)])

    own, part, tok = call(
        kernelb,
        [bq[pairs - 1]] + scattered,
        [((piece, NB), F32), ((piece, NB), BF16)],
        [(pair_piece, BF16), (pair_piece, BF16), ((piece, NB), F32), ((piece, NB), BF16)],
        2,
        order=[tok],
    )
    theirs = send(part, all_swap)

    def kernelo(y0, near, far, rh, own_p, fs_out, side_out, abuf, tbuf, rbuf, pbuf, obuf, sems):
        _, c = place()
        cp = Copies(sems)
        ins = [cp.start(y0, abuf.at[0])]
        ins.append(load_by_parity(far, near, abuf.at[1], sems.at[7]))
        ins.append(load_by_parity(near, far, abuf.at[2], sems.at[8]))
        more = [cp.start(rh, rbuf), cp.start(own_p, pbuf)]
        done = []
        for k in range(STEPS):
            ins[k].wait()
            tbuf[k] = flip(abuf[k]).astype(BF16)
            done.append(cp.start(tbuf.at[k], fs_out.at[pl.ds(k * NB, NB)]))
        wait(more)
        side = flip(rbuf[...])
        for d in all_cols:

            @pl.when(c == d)
            def _(d=d):
                base = side[d * share : (d + 1) * share]
                obuf[...] = base - pbuf[...].astype(F32) if d in owners else base

        wait(done + [cp.start(obuf, side_out)])

    solved, side, tok = call(
        kernelo,
        [y0_all, near_all, far_all, rhs, p_parts[0]],
        [((STEPS * NB, wide), BF16), ((share, NB), F32)],
        [((STEPS,) + full, BF16), ((STEPS,) + tall, BF16), (tall, BF16), ((share, NB), BF16), ((share, NB), F32)],
        9,
        order=[tok],
    )

    rest = side - sum(x.astype(F32) for x in p_got)
    total = own + theirs.astype(F32)
    sums = jnp.concatenate([total[b * row_share : (b + 1) * row_share] for b in range(cb)], axis=1)
    return (solved, jnp.transpose(rest), jnp.transpose(sums), sol)


def solution(mesh):
    placed = (P("row", "col"), P("row", None), P("row", None), P("row", None))
    return jax.shard_map(
        local,
        mesh=mesh,
        in_specs=placed,
        out_specs=(P(), P("row", "col"), P("col", "row"), P("row", None)),
        check_vma=False,
    )
```

```python
import jax
import jax.numpy as jnp
from jax import lax
from jax.experimental import pallas as pl
from jax.experimental.pallas import tpu as pltpu
from jax.sharding import PartitionSpec as P

NB = 1024
STEPS = 3
BOTH = ("row", "col")
BF16, F32 = jnp.bfloat16, jnp.float32


def nn(a, b):
    return jnp.dot(a, b, preferred_element_type=F32)


def nt(a, b):
    return lax.dot_general(a, b, (((1,), (1,)), ((), ())), preferred_element_type=F32)


def flip(x):
    return jnp.transpose(x.astype(F32))


class Copies:
    def __init__(self, sems):
        self.sems = sems
        self.used = 0

    def branch(self):
        self.used = 0

    def start(self, src, dst):
        copy = pltpu.make_async_copy(src, dst, self.sems.at[self.used])
        copy.start()
        self.used += 1
        return copy


def call(kernel, ins, outs, scratch, sems, aliases=None, limit=16, order=()):
    any_space = pl.BlockSpec(memory_space=pl.ANY)
    used, ins = len(ins), list(ins) + list(order)
    outs = list(outs) + [((8, 128), F32)]

    def body(*refs):
        n = len(ins) + len(outs)
        kernel(*refs[:used], *refs[len(ins) : n - 1], *refs[n:])

    return pl.pallas_call(
        body,
        out_shape=[jax.ShapeDtypeStruct(s, d) for s, d in outs],
        in_specs=[any_space] * len(ins),
        out_specs=[any_space] * len(outs),
        scratch_shapes=[pltpu.VMEM(s, d) for s, d in scratch] + [pltpu.SemaphoreType.DMA((sems,))],
        input_output_aliases=aliases or {},
        compiler_params=pltpu.CompilerParams(vmem_limit_bytes=limit << 20),
        cost_estimate=pl.CostEstimate(flops=0, bytes_accessed=0, transcendentals=0),
    )(*ins)


def local(factor, diag_inv, rhs, forward_values):
    rows = lax.axis_size("row")
    cols = lax.axis_size("col")
    cb = factor.shape[1] // NB
    wide = rhs.shape[1]
    assert factor.shape[0] == NB and rows % 4 == 0 and cols % 2 == 0 and rows >= 8 and cb <= 2
    share = wide // cols
    row_share = wide // rows
    piece = cb * row_share
    last = rows - 1
    pairs = rows // 2
    all_cols = range(cols)
    evens = range(0, cols, 2)
    group = lambda j: j // cb
    g0, g1, g2, g5, g6 = group(0), group(1), group(2), group(last - 2), group(last - 1)
    evens5 = [d for d in evens if d // 2 != g5 // 2]
    full, square, tall = (wide, NB), (NB, NB), (NB, wide)
    pair_piece = (2, piece, NB)

    def place():
        return lax.axis_index("row"), lax.axis_index("col")

    def send(x, pairs):
        return lax.ppermute(x, BOTH, [(a * cols + b, d * cols + e) for (a, b), (d, e) in pairs])

    def block(ref, j):
        return ref.at[:, pl.ds((j % cb) * NB, NB)]

    def multiply(q_ref, v, fac, limit):
        _, c = place()
        for b in range(cb):
            q = nn(v, fac[b])
            q = jnp.where(c * cb + b < limit, q, 0.0).astype(BF16)
            q_ref[:, :, b * row_share : (b + 1) * row_share, :] = q.reshape(pairs, 2, row_share, NB)

    def rolled(cp, buf, outs):
        _, c = place()
        return [
            cp.start(buf.at[pl.ds(pl.multiple_of(lax.rem(c + s, cols) * share, share), share)], outs[s])
            for s in all_cols
        ]

    def wait(copies):
        for o in copies:
            o.wait()

    def route(cases, shape, order=(), through=(), times=1):
        n, m = len(cases), len(through)

        def kernel(*refs):
            outs, buf, sems = refs[n + m : n + m + times], refs[-2], refs[-1]
            r, c = place()
            cp = Copies(sems)
            for (cond, _), ref in zip(cases, refs):
                cp.branch()

                @pl.when(cond(r, c))
                def _(ref=ref):
                    cp.start(ref, buf).wait()
                    wait([cp.start(buf, out) for out in outs])

        return call(
            kernel,
            [v for _, v in cases] + list(through),
            [(shape, BF16)] * times + [(x.shape, x.dtype) for x in through],
            [(shape, BF16)],
            1 + times,
            aliases={n + k: times + k for k in range(m)},
            order=order,
        )

    def at(row, col):
        return lambda r, c: (r == row) & (c == col)

    def kernel0(fac, inv, rh, fv, x_out, v_out, y_out, dbuf, lbuf, rbuf, xbuf, vbuf, sems):
        r, c = place()
        cp = Copies(sems)

        @pl.when(r == 0)
        def _():
            ins = [cp.start(rh, rbuf), cp.start(inv, dbuf)]
            ins[0].wait()
            z = flip(rbuf[...]).astype(BF16)
            ins[1].wait()
            xbuf[...] = nt(z, dbuf[...]).astype(BF16)
            own = xbuf.at[pl.ds(pl.multiple_of(c * share, share), share)]
            wait([cp.start(xbuf, x_out), cp.start(own, y_out)])

        cp.branch()

        @pl.when(r == last)
        def _():
            ins = [cp.start(fv, rbuf), cp.start(inv, dbuf)]
            for g, j in ((g6, last - 1), (g5, last - 2)):

                @pl.when(c == g)
                def _(j=j):
                    pltpu.make_async_copy(block(fac, j), lbuf, sems.at[4]).start()

            ins[0].wait()
            w = flip(rbuf[...]).astype(BF16)
            ins[1].wait()
            vbuf[...] = nn(w, dbuf[...])
            v = cp.start(vbuf, v_out)

            @pl.when((c == g6) | (c == g5))
            def _():
                pltpu.make_async_copy(block(fac, 0), lbuf, sems.at[4]).wait()
                xbuf[...] = nn(vbuf[...].astype(BF16), lbuf[...]).astype(BF16)
                cp.start(xbuf, x_out).wait()

            v.wait()

    x1, v7, y0_own, _ = call(
        kernel0,
        [factor, diag_inv, rhs, forward_values],
        [(full, BF16), (full, F32), ((share, NB), BF16)],
        [(square, BF16), (square, BF16), (tall, BF16), (full, BF16), (full, F32)],
        5,
        limit=60,
    )
    q_more = [send(x1, [((last, g6), (last - 1, d)), ((last, g5), (last - 2, d))]) for d in evens5[1:]]
    a1 = send(x1, [((0, g0), (1, g0)), ((last, g6), (last - 1, g5)), ((last, g5), (last - 2, evens5[0]))])
    a2 = send(x1, [((0, g0), (2, g0)), ((last, g6), (last - 1, evens5[0])), ((last, g5), (last - 2, g5))])
    t6_parts = [a2] + q_more
    q75_parts = [a1] + q_more
    entry = [0, 3] + [2 * d for d in range(2, pairs)]
    y0_z = {e: send(y0_own, [((0, b), (e, b)) for b in all_cols]) for e in entry[1:]}

    def kernel7(v_in, fac, *rest):
        sol_out, e_out, bq = rest[0], rest[1], rest[2 : 2 + pairs]
        fbuf, vbuf, qbuf, sbuf, zbuf, sems = rest[2 + pairs :]
        r, _ = place()
        cp = Copies(sems)

        @pl.when(r == last)
        def _():
            fs = [cp.start(fac.at[:, pl.ds(k * NB, NB)], fbuf.at[k]) for k in range(cb)]
            cp.start(v_in, vbuf).wait()
            wait(fs)
            v = vbuf[...]
            multiply(qbuf, v.astype(BF16), fbuf, last)
            done = [cp.start(qbuf.at[d], bq[d]) for d in range(pairs)]
            done.append(cp.start(qbuf.at[pl.ds(0, pairs - 2)], e_out))
            sbuf[...] = jnp.transpose(v)
            wait(done + [cp.start(sbuf, sol_out)])

        cp.branch()

        @pl.when(r < last - 2)
        def _():
            zbuf[...] = jnp.zeros_like(zbuf)
            wait([cp.start(zbuf, sol_out.at[pl.ds(k * wide, wide)]) for k in range(NB // wide)])

    sol, sevens, *bq, tok = call(
        kernel7,
        [v7, factor],
        [(tall, F32), ((pairs - 2,) + pair_piece, BF16)] + [(pair_piece, BF16)] * pairs,
        [((cb, NB, NB), BF16), (full, F32), ((pairs, 2, piece, NB), BF16), (tall, F32), ((wide, wide), F32)],
        3 + cb + pairs,
    )
    sevens = send(sevens, [((last, b), (last - 2, b)) for b in all_cols])

    y0_cases = [(lambda r, c: r == 0, y0_own)] + [(lambda r, c, e=e: r == e, v) for e, v in y0_z.items()]
    y0_in, tok = route(y0_cases, (share, NB), order=[tok])
    y0_out = send(y0_in, [((e, b), (e ^ 1, b)) for e in entry for b in all_cols])

    def kernel1(p1, fac, inv, rh, fv, x_out, *rest):
        outs, (dbuf, lbuf, rbuf, abuf, xbuf, sems) = rest[:cols], rest[cols:]
        r, c = place()
        cp = Copies(sems)

        @pl.when((r == 1) & (c == g0))
        def _():
            ins = [cp.start(rh, rbuf), cp.start(p1, abuf), cp.start(block(fac, 0), lbuf), cp.start(inv, dbuf)]
            ins[0].wait()
            z = flip(rbuf[...])
            ins[1].wait()
            ins[2].wait()
            z = z - nt(abuf[...], lbuf[...]).astype(BF16).astype(F32)
            ins[3].wait()
            xbuf[...] = nt(z.astype(BF16), dbuf[...]).astype(BF16)
            wait([cp.start(xbuf, x_out)] + rolled(cp, xbuf, outs))

        cp.branch()

        @pl.when((r == last - 1) & (c == g5))
        def _():
            ins = [cp.start(fv, rbuf), cp.start(p1, abuf), cp.start(inv, dbuf), cp.start(block(fac, last - 2), lbuf)]
            ins[0].wait()
            w = flip(rbuf[...])
            ins[1].wait()
            w = w - abuf[...].astype(F32)
            ins[2].wait()
            v = nn(w.astype(BF16), dbuf[...]).astype(BF16)
            ins[3].wait()
            xbuf[...] = nn(v, lbuf[...]).astype(BF16)
            cp.start(xbuf, x_out).wait()

    x3, *parts, tok = call(
        kernel1,
        [a1, factor, diag_inv, rhs, forward_values],
        [(full, BF16)] + [((share, NB), BF16)] * cols,
        [(square, BF16), (square, BF16), (tall, BF16), (full, BF16), (full, BF16)],
        5 + cols,
        order=[tok],
    )
    a3 = send(x3, [((1, g0), (2, g1)), ((last - 1, g5), (last - 2, g5))])
    a4 = [send(x3, [((last - 1, g5), (last - 2, d))]) for d in evens5]

    def within_chip(row, owner):
        own = [((row, owner), (row, owner ^ 1))]
        return own + [((row, d), (row, d + 1)) for d in evens if d // 2 != owner // 2]

    def kernels0(p1, p2, fac, *rest):
        more, (out, lbuf, abuf, xbuf, sems) = rest[: len(evens5) - 1], rest[len(evens5) - 1 :]
        r, c = place()
        cp = Copies(sems)

        @pl.when((r == 2) & (c == g0))
        def _():
            wait([cp.start(p2, abuf), cp.start(block(fac, 0), lbuf)])
            xbuf[...] = nt(abuf[...], lbuf[...]).astype(BF16)
            cp.start(xbuf, out).wait()

        for col, ref in zip([g5] + evens5, [p1, p2] + list(more)):
            cp.branch()

            @pl.when((r == last - 1) & (c == col))
            def _(ref=ref):
                cp.start(ref, xbuf).wait()
                cp.start(xbuf, out).wait()

    t6_even, tok = call(
        kernels0,
        [a1, a2, factor] + q_more,
        [(full, BF16)],
        [(square, BF16), (full, BF16), (full, BF16)],
        3,
        order=[tok],
    )
    s0 = t6_even if g0 == g1 else send(t6_even, [((2, g0), (2, g1))])

    t6_odd = send(t6_even, within_chip(last - 1, g5))

    def kernel2(p0, p1, fac, inv, rh, *rest):
        outs, (dbuf, lbuf, rbuf, abuf, bbuf, xbuf, sems) = rest[cols : 2 * cols], rest[2 * cols :]
        r, c = place()
        cp = Copies(sems)

        @pl.when((r == 2) & (c == g1))
        def _():
            ins = [cp.start(rh, rbuf), cp.start(p1, abuf), cp.start(block(fac, 1), lbuf), cp.start(p0, bbuf), cp.start(inv, dbuf)]
            ins[0].wait()
            z = flip(rbuf[...])
            wait(ins[1:4])
            s = nt(abuf[...], lbuf[...]) + bbuf[...].astype(F32)
            z = z - s.astype(BF16).astype(F32)
            ins[4].wait()
            xbuf[...] = nt(z.astype(BF16), dbuf[...]).astype(BF16)
            wait(rolled(cp, xbuf, outs))

    *parts, tok = call(
        kernel2,
        [s0, a3, factor, diag_inv, rhs] + parts,
        [((share, NB), BF16)] * cols,
        [(square, BF16), (square, BF16), (tall, BF16), (full, BF16), (full, BF16), (full, BF16)],
        5 + cols,
        aliases={5 + k: k for k in range(cols)},
        order=[tok],
    )
    dealt = [send(parts[s], [((1, g0), (1, (g0 + s) % cols)), ((2, g1), (2, (g1 + s) % cols))]) for s in range(1, cols)]

    def is_entry(r, c):
        return ((r % 2 == 0) & (r != 2)) | (r == 3)

    y0_mine, tok = route(
        [(is_entry, y0_in), (lambda r, c: jnp.logical_not(is_entry(r, c)), y0_out)], (share, NB), [tok]
    )

    cases = [(at(1, g0), parts[0]), (at(2, g1), parts[0])]
    for s in range(1, cols):
        cases += [(at(1, (g0 + s) % cols), dealt[s - 1]), (at(2, (g1 + s) % cols), dealt[s - 1])]
    y_own, y0_mine, tok = route(cases, (share, NB), order=[tok], through=[y0_mine])
    to_odd = list(range(1, pairs))
    to_even = [0] + list(range(2, pairs))
    y_z = [
        send(y_own, [((1, b), (2 * d + 1, b)) for b in all_cols] + [((2, b), (2 * e, b)) for b in all_cols])
        for d, e in zip(to_odd, to_even)
    ]

    y0_all = lax.all_gather(y0_mine, "col", axis=0, tiled=True)
    cases = [(lambda r, c: (r == 1) | (r == 2), y_own)]
    for d, e, v in zip(to_odd, to_even, y_z):
        cases.append((lambda r, c, d=d, e=e: (r == 2 * d + 1) | (r == 2 * e), v))
    y_mine, y_near, tok = route(cases, (share, NB), order=[tok, y0_all], times=2)
    all_swap = [((a, b), (a ^ 1, b)) for a in range(rows) for b in all_cols]
    y_other = send(y_mine, all_swap)

    i = last - 2
    slots = {d: d + 1 for d in range(pairs - 2)}
    slots.update({pairs - 1: 0, pairs - 2: pairs - 1})
    own_slots = {d: d for d in range(pairs)}

    def solve(cp, te, to, fac, inv, fv, sol_out, outs, row, to_slot, scratch, sems, more=None):
        dbuf, fbuf, rbuf, abuf, qbuf, sbuf = scratch
        _, c = place()
        has = (c == g5) | ((c % 2 == 0) & (c // 2 != g5 // 2))
        sem = sems.at[4 + cb + pairs]
        ins = [cp.start(fv, rbuf), cp.start(inv, dbuf)]
        fs = [cp.start(fac.at[:, pl.ds(k * NB, NB)], fbuf.at[k]) for k in range(cb)]
        if more is not None:
            fs.append(cp.start(*more))

        @pl.when(has)
        def _():
            pltpu.make_async_copy(te, abuf, sem).start()

        @pl.when(jnp.logical_not(has))
        def _():
            pltpu.make_async_copy(to, abuf, sem).start()

        ins[0].wait()
        w = flip(rbuf[...])
        pltpu.make_async_copy(te, abuf, sem).wait()
        w = w - abuf[...].astype(F32)
        ins[1].wait()
        v = nn(w.astype(BF16), dbuf[...])
        wait(fs)
        multiply(qbuf, v.astype(BF16), fbuf, row)
        if more is not None:
            for d in range(pairs - 2):
                qbuf[d] = (qbuf[d].astype(F32) + more[1][d].astype(F32)).astype(BF16)
        done = [cp.start(qbuf.at[d], outs[t]) for d, t in to_slot.items()]
        sbuf[...] = jnp.transpose(v)
        wait(done + [cp.start(sbuf, sol_out)])

    solve_scratch = [(square, BF16), ((cb, NB, NB), BF16), (tall, BF16), (full, BF16), ((pairs, 2, piece, NB), BF16), (tall, F32)]

    def kernelt(*refs):
        n = len(evens5) + 1
        first, second, refs = refs[:n], refs[n : 2 * n], refs[2 * n :]
        out, abuf, bbuf, sems = refs[2], refs[-3], refs[-2], refs[-1]
        r, c = place()
        cp = Copies(sems)
        for col, x, q in zip([g5] + evens5, first, second):
            cp.branch()

            @pl.when((r == last - 2) & (c == col))
            def _(x=x, q=q):
                wait([cp.start(x, abuf), cp.start(q, bbuf)])
                abuf[...] = (abuf[...].astype(F32) + bbuf[...].astype(F32)).astype(BF16)
                cp.start(abuf, out).wait()

    n_first = 2 * len(evens5) + 2
    t5_even, y_near, sevens, tok = call(
        kernelt,
        [a3] + a4 + [a2] + q75_parts + [y_near, sevens],
        [(full, BF16), ((share, NB), BF16), (sevens.shape, BF16)],
        [(full, BF16), (full, BF16)],
        3,
        aliases={n_first: 1, n_first + 1: 2},
        order=[tok],
    )
    t5_odd = send(t5_even, within_chip(last - 2, g5))

    near_all = lax.all_gather(y_near, "col", axis=0, tiled=True)

    def kernel5(t6e, t6o, t5e, t5o, seven, fac, inv, fv, *rest):
        n = pairs + 2
        sol_out, outs = rest[n], rest[n + 1 : n + 1 + pairs]
        scratch, ebuf, sems = rest[2 * n : -2], rest[-2], rest[-1]
        r, _ = place()
        cp = Copies(sems)

        @pl.when(r == last - 1)
        def _():
            solve(cp, t6e, t6o, fac, inv, fv, sol_out, outs, last - 1, own_slots, scratch, sems)

        cp.branch()

        @pl.when(r == i)
        def _():
            solve(cp, t5e, t5o, fac, inv, fv, sol_out, outs, i, slots, scratch, sems, (seven, ebuf))

    sol, *bq, y_other, tok = call(
        kernel5,
        [t6_even, t6_odd, t5_even, t5_odd, sevens, factor, diag_inv, forward_values, sol] + bq + [y_other],
        [(tall, F32)] + [(pair_piece, BF16)] * pairs + [((share, NB), BF16)],
        solve_scratch + [((pairs - 2,) + pair_piece, BF16)],
        5 + cb + pairs,
        aliases={8 + k: k for k in range(pairs + 2)},
        order=[tok, near_all],
    )
    scattered = []
    for t in range(pairs - 1):
        to = [d for d, k in slots.items() if k == t][0]
        pairs_t = [((last - 1, b), (2 * t, b)) for b in all_cols]
        pairs_t += [((last, b), (2 * t + 1, b)) for b in all_cols if t == pairs - 2]
        scattered.append(send(bq[t], pairs_t + [((i, b), (2 * to + 1, b)) for b in all_cols]))

    far_all = lax.all_gather(y_other, "col", axis=0, tiled=True)

    def load_by_parity(even, odd, buf, sem):
        r, _ = place()
        for parity, ref in enumerate((even, odd)):

            @pl.when(lax.rem(r, 2) == parity)
            def _(ref=ref):
                pltpu.make_async_copy(ref, buf, sem).start()

        return pltpu.make_async_copy(even, buf, sem)

    owners = sorted({g0, g1, g2})

    def kernelr(y0, near, far, fac, *rest):
        outs, (lbuf, abuf, pbuf, sems) = rest[:cols], rest[cols:]
        r, c = place()
        cp = Copies(sems)

        for g in owners:
            cp.branch()

            @pl.when(c == g)
            def _(g=g):
                ins = []
                if g == g0:
                    ins.append((0, cp.start(y0, abuf.at[0]), cp.start(block(fac, 0), lbuf.at[0])))
                for k, gk, even, odd in ((1, g1, far, near), (2, g2, near, far)):
                    if gk == g:
                        n = len(ins)
                        a = load_by_parity(even, odd, abuf.at[n], sems.at[4 + cols])
                        ins.append((k, a, cp.start(block(fac, k), lbuf.at[n])))
                total = None
                for n, (k, a, b) in enumerate(ins):
                    a.wait()
                    b.wait()
                    p = jnp.where(r > k, nt(abuf[n], lbuf[n]), 0.0)
                    total = p if total is None else total + p
                pbuf[...] = total.astype(BF16)
                wait(rolled(cp, pbuf, outs))

    *p_parts, tok = call(
        kernelr,
        [y0_all, near_all, far_all, factor],
        [((share, NB), BF16)] * cols,
        [((2, NB, NB), BF16), ((2,) + full, BF16), (full, BF16)],
        5 + cols,
        order=[tok],
    )
    p_got = [
        send(p_parts[s], [((a, g), (a, (g + s) % cols)) for a in range(1, rows) for g in owners]) for s in range(1, cols)
    ]

    def kernelb(own_q, *rest):
        got, (own_out, part_out, bbuf, fbuf, obuf, pbuf, sems) = rest[: pairs - 1], rest[pairs - 1 :]
        r, _ = place()
        cp = Copies(sems)
        refs = list(got) + [own_q]
        for d in range(pairs):
            cp.branch()

            @pl.when(r == 2 * d)
            def _(d=d):
                cp.start(refs[d], bbuf).wait()

            @pl.when(r == 2 * d + 1)
            def _(d=d):
                cp.start(refs[slots[d]], fbuf).wait()

        cp.branch()

        @pl.when(r == last)
        def _():
            cp.start(own_q, bbuf).wait()

        @pl.when(r == last - 2)
        def _():
            cp.start(refs[pairs - 2], bbuf).wait()

        @pl.when(lax.rem(r, 2) == 0)
        def _():
            obuf[...] = bbuf[0].astype(F32)
            pbuf[...] = bbuf[1]

        @pl.when((lax.rem(r, 2) == 1) & (r < last - 2))
        def _():
            obuf[...] = fbuf[1].astype(F32)
            pbuf[...] = fbuf[0]

        @pl.when((lax.rem(r, 2) == 1) & (r >= last - 2))
        def _():
            obuf[...] = fbuf[1].astype(F32) + bbuf[1].astype(F32)
            pbuf[...] = (fbuf[0].astype(F32) + bbuf[0].astype(F32)).astype(BF16)

        cp.branch()
        wait([cp.start(pbuf, part_out), cp.start(obuf, own_out)])

    own, part, tok = call(
        kernelb,
        [bq[pairs - 1]] + scattered,
        [((piece, NB), F32), ((piece, NB), BF16)],
        [(pair_piece, BF16), (pair_piece, BF16), ((piece, NB), F32), ((piece, NB), BF16)],
        2,
        order=[tok],
    )
    theirs = send(part, all_swap)

    def kernelo(y0, near, far, rh, own_p, fs_out, side_out, abuf, tbuf, rbuf, pbuf, obuf, sems):
        _, c = place()
        cp = Copies(sems)
        ins = [cp.start(y0, abuf.at[0])]
        ins.append(load_by_parity(far, near, abuf.at[1], sems.at[7]))
        ins.append(load_by_parity(near, far, abuf.at[2], sems.at[8]))
        more = [cp.start(rh, rbuf), cp.start(own_p, pbuf)]
        done = []
        for k in range(STEPS):
            ins[k].wait()
            tbuf[k] = flip(abuf[k]).astype(BF16)
            done.append(cp.start(tbuf.at[k], fs_out.at[pl.ds(k * NB, NB)]))
        wait(more)
        side = flip(rbuf[...])
        for d in all_cols:

            @pl.when(c == d)
            def _(d=d):
                base = side[d * share : (d + 1) * share]
                obuf[...] = base - pbuf[...].astype(F32) if d in owners else base

        wait(done + [cp.start(obuf, side_out)])

    solved, side, tok = call(
        kernelo,
        [y0_all, near_all, far_all, rhs, p_parts[0]],
        [((STEPS * NB, wide), BF16), ((share, NB), F32)],
        [((STEPS,) + full, BF16), ((STEPS,) + tall, BF16), (tall, BF16), ((share, NB), BF16), ((share, NB), F32)],
        9,
        order=[tok],
    )

    rest = side - sum(x.astype(F32) for x in p_got)
    total = own + theirs.astype(F32)
    sums = jnp.concatenate([total[b * row_share : (b + 1) * row_share] for b in range(cb)], axis=1)
    return (solved, jnp.transpose(rest), jnp.transpose(sums), sol)


def solution(mesh):
    placed = (P("row", "col"), P("row", None), P("row", None), P("row", None))
    return jax.shard_map(
        local,
        mesh=mesh,
        in_specs=placed,
        out_specs=(P(), P("row", "col"), P("col", "row"), P("row", None)),
        check_vma=False,
    )
```

```python
import jax
import jax.numpy as jnp
from jax import lax
from jax.experimental import pallas as pl
from jax.experimental.pallas import tpu as pltpu
from jax.sharding import PartitionSpec as P

NB = 1024
STEPS = 3
BOTH = ("row", "col")
BF16, F32 = jnp.bfloat16, jnp.float32


def nn(a, b):
    return jnp.dot(a, b, preferred_element_type=F32)


def nt(a, b):
    return lax.dot_general(a, b, (((1,), (1,)), ((), ())), preferred_element_type=F32)


def flip(x):
    return jnp.transpose(x).astype(F32)


class Copies:
    def __init__(self, sems):
        self.sems = sems
        self.used = 0

    def branch(self):
        self.used = 0

    def start(self, src, dst):
        copy = pltpu.make_async_copy(src, dst, self.sems.at[self.used])
        copy.start()
        self.used += 1
        return copy


def call(kernel, ins, outs, scratch, sems, aliases=None, limit=16, order=()):
    any_space = pl.BlockSpec(memory_space=pl.ANY)
    used, ins = len(ins), list(ins) + list(order)
    outs = list(outs) + [((8, 128), F32)]

    def body(*refs):
        n = len(ins) + len(outs)
        kernel(*refs[:used], *refs[len(ins) : n - 1], *refs[n:])

    return pl.pallas_call(
        body,
        out_shape=[jax.ShapeDtypeStruct(s, d) for s, d in outs],
        in_specs=[any_space] * len(ins),
        out_specs=[any_space] * len(outs),
        scratch_shapes=[pltpu.VMEM(s, d) for s, d in scratch] + [pltpu.SemaphoreType.DMA((sems,))],
        input_output_aliases=aliases or {},
        compiler_params=pltpu.CompilerParams(vmem_limit_bytes=limit << 20),
        cost_estimate=pl.CostEstimate(flops=0, bytes_accessed=0, transcendentals=0),
    )(*ins)


def local(factor, diag_inv, rhs, forward_values):
    rows = lax.axis_size("row")
    cols = lax.axis_size("col")
    cb = factor.shape[1] // NB
    wide = rhs.shape[1]
    assert factor.shape[0] == NB and rows % 4 == 0 and cols % 2 == 0 and rows >= 8 and cb <= 2
    share = wide // cols
    row_share = wide // rows
    piece = cb * row_share
    last = rows - 1
    pairs = rows // 2
    all_cols = range(cols)
    evens = range(0, cols, 2)
    group = lambda j: j // cb
    g0, g1, g2, g5, g6 = group(0), group(1), group(2), group(last - 2), group(last - 1)
    evens5 = [d for d in evens if d // 2 != g5 // 2]
    full, square, tall = (wide, NB), (NB, NB), (NB, wide)
    pair_piece = (2, piece, NB)

    def place():
        return lax.axis_index("row"), lax.axis_index("col")

    def send(x, pairs):
        return lax.ppermute(x, BOTH, [(a * cols + b, d * cols + e) for (a, b), (d, e) in pairs])

    def block(ref, j):
        return ref.at[:, pl.ds((j % cb) * NB, NB)]

    def multiply(q_ref, v, fac, limit):
        _, c = place()
        for b in range(cb):
            q = nn(v, fac[b])
            q = jnp.where(c * cb + b < limit, q, 0.0).astype(BF16)
            q_ref[:, :, b * row_share : (b + 1) * row_share, :] = q.reshape(pairs, 2, row_share, NB)

    def rolled(cp, buf, outs):
        _, c = place()
        return [
            cp.start(buf.at[pl.ds(pl.multiple_of(lax.rem(c + s, cols) * share, share), share)], outs[s])
            for s in all_cols
        ]

    def wait(copies):
        for o in copies:
            o.wait()

    def route(cases, shape, order=(), through=(), times=1):
        n, m = len(cases), len(through)

        def kernel(*refs):
            outs, buf, sems = refs[n + m : n + m + times], refs[-2], refs[-1]
            r, c = place()
            cp = Copies(sems)
            for (cond, _), ref in zip(cases, refs):
                cp.branch()

                @pl.when(cond(r, c))
                def _(ref=ref):
                    cp.start(ref, buf).wait()
                    wait([cp.start(buf, out) for out in outs])

        return call(
            kernel,
            [v for _, v in cases] + list(through),
            [(shape, BF16)] * times + [(x.shape, x.dtype) for x in through],
            [(shape, BF16)],
            1 + times,
            aliases={n + k: times + k for k in range(m)},
            order=order,
        )

    def at(row, col):
        return lambda r, c: (r == row) & (c == col)

    def kernel0(fac, inv, rh, fv, x_out, v_out, y_out, dbuf, lbuf, rbuf, xbuf, vbuf, sems):
        r, c = place()
        cp = Copies(sems)

        @pl.when(r == 0)
        def _():
            ins = [cp.start(rh, rbuf), cp.start(inv, dbuf)]
            ins[0].wait()
            z = flip(rbuf[...]).astype(BF16)
            ins[1].wait()
            xbuf[...] = nt(z, dbuf[...]).astype(BF16)
            own = xbuf.at[pl.ds(pl.multiple_of(c * share, share), share)]
            wait([cp.start(xbuf, x_out), cp.start(own, y_out)])

        cp.branch()

        @pl.when(r == last)
        def _():
            ins = [cp.start(fv, rbuf), cp.start(inv, dbuf)]
            for g, j in ((g6, last - 1), (g5, last - 2)):

                @pl.when(c == g)
                def _(j=j):
                    pltpu.make_async_copy(block(fac, j), lbuf, sems.at[4]).start()

            ins[0].wait()
            w = flip(rbuf[...]).astype(BF16)
            ins[1].wait()
            vbuf[...] = nn(w, dbuf[...])
            v = cp.start(vbuf, v_out)

            @pl.when((c == g6) | (c == g5))
            def _():
                pltpu.make_async_copy(block(fac, 0), lbuf, sems.at[4]).wait()
                xbuf[...] = nn(vbuf[...].astype(BF16), lbuf[...]).astype(BF16)
                cp.start(xbuf, x_out).wait()

            v.wait()

    x1, v7, y0_own, _ = call(
        kernel0,
        [factor, diag_inv, rhs, forward_values],
        [(full, BF16), (full, F32), ((share, NB), BF16)],
        [(square, BF16), (square, BF16), (tall, BF16), (full, BF16), (full, F32)],
        5,
        limit=60,
    )
    q_more = [send(x1, [((last, g6), (last - 1, d)), ((last, g5), (last - 2, d))]) for d in evens5[1:]]
    a1 = send(x1, [((0, g0), (1, g0)), ((last, g6), (last - 1, g5)), ((last, g5), (last - 2, evens5[0]))])
    a2 = send(x1, [((0, g0), (2, g0)), ((last, g6), (last - 1, evens5[0])), ((last, g5), (last - 2, g5))])
    t6_parts = [a2] + q_more
    q75_parts = [a1] + q_more
    entry = [0, 3] + [2 * d for d in range(2, pairs)]
    y0_z = {e: send(y0_own, [((0, b), (e, b)) for b in all_cols]) for e in entry[1:]}

    def kernel7(v_in, fac, *rest):
        sol_out, e_out, bq = rest[0], rest[1], rest[2 : 2 + pairs]
        fbuf, vbuf, qbuf, sbuf, zbuf, sems = rest[2 + pairs :]
        r, _ = place()
        cp = Copies(sems)

        @pl.when(r == last)
        def _():
            fs = [cp.start(fac.at[:, pl.ds(k * NB, NB)], fbuf.at[k]) for k in range(cb)]
            cp.start(v_in, vbuf).wait()
            wait(fs)
            v = vbuf[...]
            multiply(qbuf, v.astype(BF16), fbuf, last)
            done = [cp.start(qbuf.at[d], bq[d]) for d in range(pairs)]
            done.append(cp.start(qbuf.at[pl.ds(0, pairs - 1)], e_out))
            sbuf[...] = jnp.transpose(v)
            wait(done + [cp.start(sbuf, sol_out)])

        cp.branch()

        @pl.when(r < last - 2)
        def _():
            zbuf[...] = jnp.zeros_like(zbuf)
            wait([cp.start(zbuf, sol_out.at[pl.ds(k * wide, wide)]) for k in range(NB // wide)])

    sol, sevens, *bq, tok = call(
        kernel7,
        [v7, factor],
        [(tall, F32), ((pairs - 1,) + pair_piece, BF16)] + [(pair_piece, BF16)] * pairs,
        [((cb, NB, NB), BF16), (full, F32), ((pairs, 2, piece, NB), BF16), (tall, F32), ((wide, wide), F32)],
        3 + cb + pairs,
    )
    sevens = send(sevens, [((last, b), (last - 2, b)) for b in all_cols])

    y0_cases = [(lambda r, c: r == 0, y0_own)] + [(lambda r, c, e=e: r == e, v) for e, v in y0_z.items()]
    y0_in, tok = route(y0_cases, (share, NB), order=[tok])
    y0_out = send(y0_in, [((e, b), (e ^ 1, b)) for e in entry for b in all_cols])

    def kernel1(p1, fac, inv, rh, fv, x_out, *rest):
        outs, (dbuf, lbuf, rbuf, abuf, xbuf, sems) = rest[:cols], rest[cols:]
        r, c = place()
        cp = Copies(sems)

        @pl.when((r == 1) & (c == g0))
        def _():
            ins = [cp.start(rh, rbuf), cp.start(p1, abuf), cp.start(block(fac, 0), lbuf), cp.start(inv, dbuf)]
            ins[0].wait()
            z = flip(rbuf[...])
            ins[1].wait()
            ins[2].wait()
            z = z - nt(abuf[...], lbuf[...]).astype(BF16).astype(F32)
            ins[3].wait()
            xbuf[...] = nt(z.astype(BF16), dbuf[...]).astype(BF16)
            wait([cp.start(xbuf, x_out)] + rolled(cp, xbuf, outs))

        cp.branch()

        @pl.when((r == last - 1) & (c == g5))
        def _():
            ins = [cp.start(fv, rbuf), cp.start(p1, abuf), cp.start(inv, dbuf), cp.start(block(fac, last - 2), lbuf)]
            ins[0].wait()
            w = flip(rbuf[...])
            ins[1].wait()
            w = w - abuf[...].astype(F32)
            ins[2].wait()
            v = nn(w.astype(BF16), dbuf[...]).astype(BF16)
            ins[3].wait()
            xbuf[...] = nn(v, lbuf[...]).astype(BF16)
            cp.start(xbuf, x_out).wait()

    x3, *parts, tok = call(
        kernel1,
        [a1, factor, diag_inv, rhs, forward_values],
        [(full, BF16)] + [((share, NB), BF16)] * cols,
        [(square, BF16), (square, BF16), (tall, BF16), (full, BF16), (full, BF16)],
        5 + cols,
        order=[tok],
    )
    a3 = send(x3, [((1, g0), (2, g1)), ((last - 1, g5), (last - 2, g5))])
    a4 = [send(x3, [((last - 1, g5), (last - 2, d))]) for d in evens5]

    def within_chip(row, owner):
        own = [((row, owner), (row, owner ^ 1))]
        return own + [((row, d), (row, d + 1)) for d in evens if d // 2 != owner // 2]

    def kernels0(p1, p2, fac, *rest):
        more, (out, lbuf, abuf, xbuf, sems) = rest[: len(evens5) - 1], rest[len(evens5) - 1 :]
        r, c = place()
        cp = Copies(sems)

        @pl.when((r == 2) & (c == g0))
        def _():
            wait([cp.start(p2, abuf), cp.start(block(fac, 0), lbuf)])
            xbuf[...] = nt(abuf[...], lbuf[...]).astype(BF16)
            cp.start(xbuf, out).wait()

        for col, ref in zip([g5] + evens5, [p1, p2] + list(more)):
            cp.branch()

            @pl.when((r == last - 1) & (c == col))
            def _(ref=ref):
                cp.start(ref, xbuf).wait()
                cp.start(xbuf, out).wait()

    t6_even, tok = call(
        kernels0,
        [a1, a2, factor] + q_more,
        [(full, BF16)],
        [(square, BF16), (full, BF16), (full, BF16)],
        3,
        order=[tok],
    )
    s0 = t6_even if g0 == g1 else send(t6_even, [((2, g0), (2, g1))])

    t6_odd = send(t6_even, within_chip(last - 1, g5))

    def kernel2(p0, p1, fac, inv, rh, *rest):
        outs, (dbuf, lbuf, rbuf, abuf, bbuf, xbuf, sems) = rest[cols : 2 * cols], rest[2 * cols :]
        r, c = place()
        cp = Copies(sems)

        @pl.when((r == 2) & (c == g1))
        def _():
            ins = [cp.start(rh, rbuf), cp.start(p1, abuf), cp.start(block(fac, 1), lbuf), cp.start(p0, bbuf), cp.start(inv, dbuf)]
            ins[0].wait()
            z = flip(rbuf[...])
            wait(ins[1:4])
            s = nt(abuf[...], lbuf[...]) + bbuf[...].astype(F32)
            z = z - s.astype(BF16).astype(F32)
            ins[4].wait()
            xbuf[...] = nt(z.astype(BF16), dbuf[...]).astype(BF16)
            wait(rolled(cp, xbuf, outs))

    *parts, tok = call(
        kernel2,
        [s0, a3, factor, diag_inv, rhs] + parts,
        [((share, NB), BF16)] * cols,
        [(square, BF16), (square, BF16), (tall, BF16), (full, BF16), (full, BF16), (full, BF16)],
        5 + cols,
        aliases={5 + k: k for k in range(cols)},
        order=[tok],
    )
    dealt = [send(parts[s], [((1, g0), (1, (g0 + s) % cols)), ((2, g1), (2, (g1 + s) % cols))]) for s in range(1, cols)]

    def is_entry(r, c):
        return ((r % 2 == 0) & (r != 2)) | (r == 3)

    y0_mine, tok = route(
        [(is_entry, y0_in), (lambda r, c: jnp.logical_not(is_entry(r, c)), y0_out)], (share, NB), [tok]
    )

    cases = [(at(1, g0), parts[0]), (at(2, g1), parts[0])]
    for s in range(1, cols):
        cases += [(at(1, (g0 + s) % cols), dealt[s - 1]), (at(2, (g1 + s) % cols), dealt[s - 1])]
    y_own, y0_mine, tok = route(cases, (share, NB), order=[tok], through=[y0_mine])
    to_odd = list(range(1, pairs))
    to_even = [0] + list(range(2, pairs))
    y_z = [
        send(y_own, [((1, b), (2 * d + 1, b)) for b in all_cols] + [((2, b), (2 * e, b)) for b in all_cols])
        for d, e in zip(to_odd, to_even)
    ]

    y0_all = lax.all_gather(y0_mine, "col", axis=0, tiled=True)
    cases = [(lambda r, c: (r == 1) | (r == 2), y_own)]
    for d, e, v in zip(to_odd, to_even, y_z):
        cases.append((lambda r, c, d=d, e=e: (r == 2 * d + 1) | (r == 2 * e), v))
    y_mine, y_near, tok = route(cases, (share, NB), order=[tok, y0_all], times=2)
    all_swap = [((a, b), (a ^ 1, b)) for a in range(rows) for b in all_cols]
    y_other = send(y_mine, all_swap)

    i = last - 2
    slots = {d: d + 1 for d in range(pairs - 2)}
    slots.update({pairs - 1: 0, pairs - 2: pairs - 1})
    own_slots = {d: d for d in range(pairs)}

    def solve(cp, te, to, fac, inv, fv, sol_out, outs, row, to_slot, scratch, sems, more=None):
        dbuf, fbuf, rbuf, abuf, qbuf, sbuf = scratch
        _, c = place()
        has = (c == g5) | ((c % 2 == 0) & (c // 2 != g5 // 2))
        sem = sems.at[4 + cb + pairs]
        ins = [cp.start(fv, rbuf), cp.start(inv, dbuf)]
        fs = [cp.start(fac.at[:, pl.ds(k * NB, NB)], fbuf.at[k]) for k in range(cb)]
        if more is not None:
            fs.append(cp.start(*more))

        @pl.when(has)
        def _():
            pltpu.make_async_copy(te, abuf, sem).start()

        @pl.when(jnp.logical_not(has))
        def _():
            pltpu.make_async_copy(to, abuf, sem).start()

        ins[0].wait()
        w = flip(rbuf[...])
        pltpu.make_async_copy(te, abuf, sem).wait()
        w = w - abuf[...].astype(F32)
        ins[1].wait()
        v = nn(w.astype(BF16), dbuf[...])
        wait(fs)
        multiply(qbuf, v.astype(BF16), fbuf, row)
        if more is not None:
            for d in range(pairs - 1):
                qbuf[d] = (qbuf[d].astype(F32) + more[1][d].astype(F32)).astype(BF16)
        done = [cp.start(qbuf.at[d], outs[t]) for d, t in to_slot.items()]
        sbuf[...] = jnp.transpose(v)
        wait(done + [cp.start(sbuf, sol_out)])

    solve_scratch = [(square, BF16), ((cb, NB, NB), BF16), (tall, BF16), (full, BF16), ((pairs, 2, piece, NB), BF16), (tall, F32)]

    def kernelt(*refs):
        n = len(evens5) + 1
        first, second, refs = refs[:n], refs[n : 2 * n], refs[2 * n :]
        out, abuf, bbuf, sems = refs[2], refs[-3], refs[-2], refs[-1]
        r, c = place()
        cp = Copies(sems)
        for col, x, q in zip([g5] + evens5, first, second):
            cp.branch()

            @pl.when((r == last - 2) & (c == col))
            def _(x=x, q=q):
                wait([cp.start(x, abuf), cp.start(q, bbuf)])
                abuf[...] = (abuf[...].astype(F32) + bbuf[...].astype(F32)).astype(BF16)
                cp.start(abuf, out).wait()

    n_first = 2 * len(evens5) + 2
    t5_even, y_near, sevens, tok = call(
        kernelt,
        [a3] + a4 + [a2] + q75_parts + [y_near, sevens],
        [(full, BF16), ((share, NB), BF16), (sevens.shape, BF16)],
        [(full, BF16), (full, BF16)],
        3,
        aliases={n_first: 1, n_first + 1: 2},
        order=[tok],
    )
    t5_odd = send(t5_even, within_chip(last - 2, g5))

    near_all = lax.all_gather(y_near, "col", axis=0, tiled=True)

    def kernel5(t6e, t6o, t5e, t5o, seven, fac, inv, fv, *rest):
        n = pairs + 2
        sol_out, outs = rest[n], rest[n + 1 : n + 1 + pairs]
        scratch, ebuf, sems = rest[2 * n : -2], rest[-2], rest[-1]
        r, _ = place()
        cp = Copies(sems)

        @pl.when(r == last - 1)
        def _():
            solve(cp, t6e, t6o, fac, inv, fv, sol_out, outs, last - 1, own_slots, scratch, sems)

        cp.branch()

        @pl.when(r == i)
        def _():
            solve(cp, t5e, t5o, fac, inv, fv, sol_out, outs, i, slots, scratch, sems, (seven, ebuf))

    sol, *bq, y_other, tok = call(
        kernel5,
        [t6_even, t6_odd, t5_even, t5_odd, sevens, factor, diag_inv, forward_values, sol] + bq + [y_other],
        [(tall, F32)] + [(pair_piece, BF16)] * pairs + [((share, NB), BF16)],
        solve_scratch + [((pairs - 1,) + pair_piece, BF16)],
        5 + cb + pairs,
        aliases={8 + k: k for k in range(pairs + 2)},
        order=[tok, near_all],
    )
    scattered = []
    for t in range(pairs - 1):
        to = [d for d, k in slots.items() if k == t][0]
        pairs_t = [((last - 1, b), (2 * t, b)) for b in all_cols]
        scattered.append(send(bq[t], pairs_t + [((i, b), (2 * to + 1, b)) for b in all_cols]))

    far_all = lax.all_gather(y_other, "col", axis=0, tiled=True)

    def load_by_parity(even, odd, buf, sem):
        r, _ = place()
        for parity, ref in enumerate((even, odd)):

            @pl.when(lax.rem(r, 2) == parity)
            def _(ref=ref):
                pltpu.make_async_copy(ref, buf, sem).start()

        return pltpu.make_async_copy(even, buf, sem)

    owners = sorted({g0, g1, g2})

    def kernelr(y0, near, far, fac, *rest):
        outs, (lbuf, abuf, pbuf, sems) = rest[:cols], rest[cols:]
        r, c = place()
        cp = Copies(sems)

        for g in owners:
            cp.branch()

            @pl.when(c == g)
            def _(g=g):
                ins = []
                if g == g0:
                    ins.append((0, cp.start(y0, abuf.at[0]), cp.start(block(fac, 0), lbuf.at[0])))
                for k, gk, even, odd in ((1, g1, far, near), (2, g2, near, far)):
                    if gk == g:
                        n = len(ins)
                        a = load_by_parity(even, odd, abuf.at[n], sems.at[4 + cols])
                        ins.append((k, a, cp.start(block(fac, k), lbuf.at[n])))
                total = None
                for n, (k, a, b) in enumerate(ins):
                    a.wait()
                    b.wait()
                    p = jnp.where(r > k, nt(abuf[n], lbuf[n]), 0.0)
                    total = p if total is None else total + p
                pbuf[...] = total.astype(BF16)
                wait(rolled(cp, pbuf, outs))

    *p_parts, tok = call(
        kernelr,
        [y0_all, near_all, far_all, factor],
        [((share, NB), BF16)] * cols,
        [((2, NB, NB), BF16), ((2,) + full, BF16), (full, BF16)],
        5 + cols,
        order=[tok],
    )
    p_got = [
        send(p_parts[s], [((a, g), (a, (g + s) % cols)) for a in range(1, rows) for g in owners]) for s in range(1, cols)
    ]

    def kernelb(own_q, *rest):
        got, (own_out, part_out, bbuf, fbuf, obuf, pbuf, sems) = rest[: pairs - 1], rest[pairs - 1 :]
        r, _ = place()
        cp = Copies(sems)
        refs = list(got) + [own_q]
        for d in range(pairs):
            cp.branch()

            @pl.when(r == 2 * d)
            def _(d=d):
                cp.start(refs[d], bbuf).wait()

            @pl.when(r == 2 * d + 1)
            def _(d=d):
                cp.start(refs[slots[d]], fbuf).wait()

        cp.branch()

        @pl.when(r == last)
        def _():
            cp.start(own_q, bbuf).wait()

        @pl.when(lax.rem(r, 2) == 0)
        def _():
            obuf[...] = bbuf[0].astype(F32)
            pbuf[...] = bbuf[1]

        @pl.when((lax.rem(r, 2) == 1) & (r < last))
        def _():
            obuf[...] = fbuf[1].astype(F32)
            pbuf[...] = fbuf[0]

        @pl.when(r == last)
        def _():
            obuf[...] = fbuf[1].astype(F32) + bbuf[1].astype(F32)
            pbuf[...] = (fbuf[0].astype(F32) + bbuf[0].astype(F32)).astype(BF16)

        cp.branch()
        wait([cp.start(pbuf, part_out), cp.start(obuf, own_out)])

    own, part, tok = call(
        kernelb,
        [bq[pairs - 1]] + scattered,
        [((piece, NB), F32), ((piece, NB), BF16)],
        [(pair_piece, BF16), (pair_piece, BF16), ((piece, NB), F32), ((piece, NB), BF16)],
        2,
        order=[tok],
    )
    theirs = send(part, all_swap)

    def kernelo(y0, near, far, rh, own_p, fs_out, side_out, abuf, tbuf, rbuf, pbuf, obuf, sems):
        _, c = place()
        cp = Copies(sems)
        ins = [cp.start(y0, abuf.at[0])]
        ins.append(load_by_parity(far, near, abuf.at[1], sems.at[7]))
        ins.append(load_by_parity(near, far, abuf.at[2], sems.at[8]))
        more = [cp.start(rh, rbuf), cp.start(own_p, pbuf)]
        done = []
        for k in range(STEPS):
            ins[k].wait()
            tbuf[k] = flip(abuf[k]).astype(BF16)
            done.append(cp.start(tbuf.at[k], fs_out.at[pl.ds(k * NB, NB)]))
        wait(more)
        side = flip(rbuf[...])
        for d in all_cols:

            @pl.when(c == d)
            def _(d=d):
                base = side[d * share : (d + 1) * share]
                obuf[...] = base - pbuf[...].astype(F32) if d in owners else base

        wait(done + [cp.start(obuf, side_out)])

    solved, side, tok = call(
        kernelo,
        [y0_all, near_all, far_all, rhs, p_parts[0]],
        [((STEPS * NB, wide), BF16), ((share, NB), F32)],
        [((STEPS,) + full, BF16), ((STEPS,) + tall, BF16), (tall, BF16), ((share, NB), BF16), ((share, NB), F32)],
        9,
        order=[tok],
    )

    rest = side - sum(x.astype(F32) for x in p_got)
    total = own + theirs.astype(F32)
    sums = jnp.concatenate([total[b * row_share : (b + 1) * row_share] for b in range(cb)], axis=1)
    return (solved, jnp.transpose(rest), jnp.transpose(sums), sol)


def solution(mesh):
    placed = (P("row", "col"), P("row", None), P("row", None), P("row", None))
    return jax.shard_map(
        local,
        mesh=mesh,
        in_specs=placed,
        out_specs=(P(), P("row", "col"), P("col", "row"), P("row", None)),
        check_vma=False,
    )
```

```python
import jax
import jax.numpy as jnp
from jax import lax
from jax.experimental import pallas as pl
from jax.experimental.pallas import tpu as pltpu
from jax.sharding import PartitionSpec as P

NB = 1024
STEPS = 3
BOTH = ("row", "col")
BF16, F32 = jnp.bfloat16, jnp.float32


def nn(a, b):
    return jnp.dot(a, b, preferred_element_type=F32)


def nt(a, b):
    return lax.dot_general(a, b, (((1,), (1,)), ((), ())), preferred_element_type=F32)


def flip(x):
    return jnp.transpose(x).astype(F32)


class Copies:
    def __init__(self, sems):
        self.sems = sems
        self.used = 0

    def branch(self):
        self.used = 0

    def start(self, src, dst):
        copy = pltpu.make_async_copy(src, dst, self.sems.at[self.used])
        copy.start()
        self.used += 1
        return copy


def call(kernel, ins, outs, scratch, sems, aliases=None, limit=16, order=()):
    any_space = pl.BlockSpec(memory_space=pl.ANY)
    used, ins = len(ins), list(ins) + list(order)
    outs = list(outs) + [((8, 128), F32)]

    def body(*refs):
        n = len(ins) + len(outs)
        kernel(*refs[:used], *refs[len(ins) : n - 1], *refs[n:])

    return pl.pallas_call(
        body,
        out_shape=[jax.ShapeDtypeStruct(s, d) for s, d in outs],
        in_specs=[any_space] * len(ins),
        out_specs=[any_space] * len(outs),
        scratch_shapes=[pltpu.VMEM(s, d) for s, d in scratch] + [pltpu.SemaphoreType.DMA((sems,))],
        input_output_aliases=aliases or {},
        compiler_params=pltpu.CompilerParams(vmem_limit_bytes=limit << 20),
        cost_estimate=pl.CostEstimate(flops=0, bytes_accessed=0, transcendentals=0),
    )(*ins)


def local(factor, diag_inv, rhs, forward_values):
    rows = lax.axis_size("row")
    cols = lax.axis_size("col")
    cb = factor.shape[1] // NB
    wide = rhs.shape[1]
    assert factor.shape[0] == NB and rows % 4 == 0 and cols % 2 == 0 and rows >= 8 and cb <= 2
    share = wide // cols
    row_share = wide // rows
    piece = cb * row_share
    last = rows - 1
    pairs = rows // 2
    all_cols = range(cols)
    evens = range(0, cols, 2)
    group = lambda j: j // cb
    g0, g1, g2, g5, g6 = group(0), group(1), group(2), group(last - 2), group(last - 1)
    evens5 = [d for d in evens if d // 2 != g5 // 2]
    full, square, tall = (wide, NB), (NB, NB), (NB, wide)
    pair_piece = (2, piece, NB)

    def place():
        return lax.axis_index("row"), lax.axis_index("col")

    def send(x, pairs):
        return lax.ppermute(x, BOTH, [(a * cols + b, d * cols + e) for (a, b), (d, e) in pairs])

    def block(ref, j):
        return ref.at[:, pl.ds((j % cb) * NB, NB)]

    def multiply(q_ref, v, fac, limit):
        _, c = place()
        for b in range(cb):
            q = nn(v, fac[b])
            q = jnp.where(c * cb + b < limit, q, 0.0).astype(BF16)
            q_ref[:, :, b * row_share : (b + 1) * row_share, :] = q.reshape(pairs, 2, row_share, NB)

    def rolled(cp, buf, outs):
        _, c = place()
        return [
            cp.start(buf.at[pl.ds(pl.multiple_of(lax.rem(c + s, cols) * share, share), share)], outs[s])
            for s in all_cols
        ]

    def wait(copies):
        for o in copies:
            o.wait()

    def route(cases, shape, order=(), through=(), times=1):
        n, m = len(cases), len(through)

        def kernel(*refs):
            outs, buf, sems = refs[n + m : n + m + times], refs[-2], refs[-1]
            r, c = place()
            cp = Copies(sems)
            for (cond, _), ref in zip(cases, refs):
                cp.branch()

                @pl.when(cond(r, c))
                def _(ref=ref):
                    cp.start(ref, buf).wait()
                    wait([cp.start(buf, out) for out in outs])

        return call(
            kernel,
            [v for _, v in cases] + list(through),
            [(shape, BF16)] * times + [(x.shape, x.dtype) for x in through],
            [(shape, BF16)],
            1 + times,
            aliases={n + k: times + k for k in range(m)},
            order=order,
        )

    def at(row, col):
        return lambda r, c: (r == row) & (c == col)

    def kernel0(fac, inv, rh, fv, x_out, v_out, y_out, dbuf, lbuf, rbuf, xbuf, vbuf, sems):
        r, c = place()
        cp = Copies(sems)

        @pl.when(r == 0)
        def _():
            ins = [cp.start(rh, rbuf), cp.start(inv, dbuf)]
            ins[0].wait()
            z = flip(rbuf[...]).astype(BF16)
            ins[1].wait()
            xbuf[...] = nt(z, dbuf[...]).astype(BF16)
            own = xbuf.at[pl.ds(pl.multiple_of(c * share, share), share)]
            wait([cp.start(xbuf, x_out), cp.start(own, y_out)])

        cp.branch()

        @pl.when(r == last)
        def _():
            ins = [cp.start(fv, rbuf), cp.start(inv, dbuf)]
            for g, j in ((g6, last - 1), (g5, last - 2)):

                @pl.when(c == g)
                def _(j=j):
                    pltpu.make_async_copy(block(fac, j), lbuf, sems.at[4]).start()

            ins[0].wait()
            w = flip(rbuf[...]).astype(BF16)
            ins[1].wait()
            vbuf[...] = nn(w, dbuf[...])
            v = cp.start(vbuf, v_out)

            @pl.when((c == g6) | (c == g5))
            def _():
                pltpu.make_async_copy(block(fac, 0), lbuf, sems.at[4]).wait()
                xbuf[...] = nn(vbuf[...].astype(BF16), lbuf[...]).astype(BF16)
                cp.start(xbuf, x_out).wait()

            v.wait()

    x1, v7, y0_own, _ = call(
        kernel0,
        [factor, diag_inv, rhs, forward_values],
        [(full, BF16), (full, F32), ((share, NB), BF16)],
        [(square, BF16), (square, BF16), (tall, BF16), (full, BF16), (full, F32)],
        5,
        limit=60,
    )
    q_more = [send(x1, [((last, g6), (last - 1, d)), ((last, g5), (last - 2, d))]) for d in evens5[1:]]
    a1 = send(x1, [((0, g0), (1, g0)), ((last, g6), (last - 1, g5)), ((last, g5), (last - 2, evens5[0]))])
    a2 = send(x1, [((0, g0), (2, g0)), ((last, g6), (last - 1, evens5[0])), ((last, g5), (last - 2, g5))])
    t6_parts = [a2] + q_more
    q75_parts = [a1] + q_more
    entry = [0, 3] + [2 * d for d in range(2, pairs)]
    y0_z = {e: send(y0_own, [((0, b), (e, b)) for b in all_cols]) for e in entry[1:]}

    def kernel7(v_in, fac, *rest):
        sol_out, e_out, bq = rest[0], rest[1], rest[2 : 2 + pairs]
        fbuf, vbuf, qbuf, sbuf, zbuf, sems = rest[2 + pairs :]
        r, _ = place()
        cp = Copies(sems)

        @pl.when(r == last)
        def _():
            fs = [cp.start(fac.at[:, pl.ds(k * NB, NB)], fbuf.at[k]) for k in range(cb)]
            cp.start(v_in, vbuf).wait()
            wait(fs)
            v = vbuf[...]
            multiply(qbuf, v.astype(BF16), fbuf, last)
            done = [cp.start(qbuf.at[d], bq[d]) for d in range(pairs)]
            done.append(cp.start(qbuf.at[pl.ds(0, pairs - 1)], e_out))
            sbuf[...] = jnp.transpose(v)
            wait(done + [cp.start(sbuf, sol_out)])

        cp.branch()

        @pl.when(r < last - 2)
        def _():
            zbuf[...] = jnp.zeros_like(zbuf)
            wait([cp.start(zbuf, sol_out.at[pl.ds(k * wide, wide)]) for k in range(NB // wide)])

    sol, sevens, *bq, tok = call(
        kernel7,
        [v7, factor],
        [(tall, F32), ((pairs - 1,) + pair_piece, BF16)] + [(pair_piece, BF16)] * pairs,
        [((cb, NB, NB), BF16), (full, F32), ((pairs, 2, piece, NB), BF16), (tall, F32), ((wide, wide), F32)],
        3 + cb + pairs,
    )
    sevens = send(sevens, [((last, b), (last - 2, b)) for b in all_cols])

    y0_cases = [(lambda r, c: r == 0, y0_own)] + [(lambda r, c, e=e: r == e, v) for e, v in y0_z.items()]
    y0_in, tok = route(y0_cases, (share, NB), order=[tok])
    y0_out = send(y0_in, [((e, b), (e ^ 1, b)) for e in entry for b in all_cols])

    def kernel1(p1, fac, inv, rh, fv, x_out, *rest):
        outs, (dbuf, lbuf, rbuf, abuf, xbuf, sems) = rest[:cols], rest[cols:]
        r, c = place()
        cp = Copies(sems)

        @pl.when((r == 1) & (c == g0))
        def _():
            ins = [cp.start(rh, rbuf), cp.start(p1, abuf), cp.start(block(fac, 0), lbuf), cp.start(inv, dbuf)]
            ins[0].wait()
            z = flip(rbuf[...])
            ins[1].wait()
            ins[2].wait()
            z = z - nt(abuf[...], lbuf[...]).astype(BF16).astype(F32)
            ins[3].wait()
            xbuf[...] = nt(z.astype(BF16), dbuf[...]).astype(BF16)
            wait([cp.start(xbuf, x_out)] + rolled(cp, xbuf, outs))

        cp.branch()

        @pl.when((r == last - 1) & (c == g5))
        def _():
            ins = [cp.start(fv, rbuf), cp.start(p1, abuf), cp.start(inv, dbuf), cp.start(block(fac, last - 2), lbuf)]
            ins[0].wait()
            w = flip(rbuf[...])
            ins[1].wait()
            w = w - abuf[...].astype(F32)
            ins[2].wait()
            v = nn(w.astype(BF16), dbuf[...]).astype(BF16)
            ins[3].wait()
            xbuf[...] = nn(v, lbuf[...]).astype(BF16)
            cp.start(xbuf, x_out).wait()

    x3, *parts, tok = call(
        kernel1,
        [a1, factor, diag_inv, rhs, forward_values],
        [(full, BF16)] + [((share, NB), BF16)] * cols,
        [(square, BF16), (square, BF16), (tall, BF16), (full, BF16), (full, BF16)],
        5 + cols,
        order=[tok],
    )
    a3 = send(x3, [((1, g0), (2, g1)), ((last - 1, g5), (last - 2, g5))])
    a4 = [send(x3, [((last - 1, g5), (last - 2, d))]) for d in evens5]

    def within_chip(row, owner):
        own = [((row, owner), (row, owner ^ 1))]
        return own + [((row, d), (row, d + 1)) for d in evens if d // 2 != owner // 2]

    def kernels0(p1, p2, fac, *rest):
        more, (out, lbuf, abuf, xbuf, sems) = rest[: len(evens5) - 1], rest[len(evens5) - 1 :]
        r, c = place()
        cp = Copies(sems)

        @pl.when((r == 2) & (c == g0))
        def _():
            wait([cp.start(p2, abuf), cp.start(block(fac, 0), lbuf)])
            xbuf[...] = nt(abuf[...], lbuf[...]).astype(BF16)
            cp.start(xbuf, out).wait()

        for col, ref in zip([g5] + evens5, [p1, p2] + list(more)):
            cp.branch()

            @pl.when((r == last - 1) & (c == col))
            def _(ref=ref):
                cp.start(ref, xbuf).wait()
                cp.start(xbuf, out).wait()

    t6_even, tok = call(
        kernels0,
        [a1, a2, factor] + q_more,
        [(full, BF16)],
        [(square, BF16), (full, BF16), (full, BF16)],
        3,
        order=[tok],
    )
    s0 = t6_even if g0 == g1 else send(t6_even, [((2, g0), (2, g1))])

    t6_odd = send(t6_even, within_chip(last - 1, g5))

    def kernel2(p0, p1, fac, inv, rh, *rest):
        outs, (dbuf, lbuf, rbuf, abuf, bbuf, xbuf, sems) = rest[cols : 2 * cols], rest[2 * cols :]
        r, c = place()
        cp = Copies(sems)

        @pl.when((r == 2) & (c == g1))
        def _():
            ins = [cp.start(rh, rbuf), cp.start(p1, abuf), cp.start(block(fac, 1), lbuf), cp.start(p0, bbuf), cp.start(inv, dbuf)]
            ins[0].wait()
            z = flip(rbuf[...])
            wait(ins[1:4])
            s = nt(abuf[...], lbuf[...]) + bbuf[...].astype(F32)
            z = z - s.astype(BF16).astype(F32)
            ins[4].wait()
            xbuf[...] = nt(z.astype(BF16), dbuf[...]).astype(BF16)
            wait(rolled(cp, xbuf, outs))

    *parts, tok = call(
        kernel2,
        [s0, a3, factor, diag_inv, rhs] + parts,
        [((share, NB), BF16)] * cols,
        [(square, BF16), (square, BF16), (tall, BF16), (full, BF16), (full, BF16), (full, BF16)],
        5 + cols,
        aliases={5 + k: k for k in range(cols)},
        order=[tok],
    )
    dealt = [send(parts[s], [((1, g0), (1, (g0 + s) % cols)), ((2, g1), (2, (g1 + s) % cols))]) for s in range(1, cols)]

    def is_entry(r, c):
        return ((r % 2 == 0) & (r != 2)) | (r == 3)

    y0_mine, tok = route(
        [(is_entry, y0_in), (lambda r, c: jnp.logical_not(is_entry(r, c)), y0_out)], (share, NB), [tok]
    )

    cases = [(at(1, g0), parts[0]), (at(2, g1), parts[0])]
    for s in range(1, cols):
        cases += [(at(1, (g0 + s) % cols), dealt[s - 1]), (at(2, (g1 + s) % cols), dealt[s - 1])]
    y_own, y0_mine, tok = route(cases, (share, NB), order=[tok], through=[y0_mine])
    to_odd = list(range(1, pairs))
    to_even = [0] + list(range(2, pairs))
    y_z = [
        send(y_own, [((1, b), (2 * d + 1, b)) for b in all_cols] + [((2, b), (2 * e, b)) for b in all_cols])
        for d, e in zip(to_odd, to_even)
    ]

    y0_all = lax.all_gather(y0_mine, "col", axis=0, tiled=True)
    cases = [(lambda r, c: (r == 1) | (r == 2), y_own)]
    for d, e, v in zip(to_odd, to_even, y_z):
        cases.append((lambda r, c, d=d, e=e: (r == 2 * d + 1) | (r == 2 * e), v))
    y_mine, y_near, tok = route(cases, (share, NB), order=[tok, y0_all], times=2)
    all_swap = [((a, b), (a ^ 1, b)) for a in range(rows) for b in all_cols]
    y_other = send(y_mine, all_swap)

    i = last - 2
    slots = {d: d + 1 for d in range(pairs - 2)}
    slots.update({pairs - 1: 0, pairs - 2: pairs - 1})
    own_slots = {d: d for d in range(pairs)}

    def solve(cp, te, to, fac, inv, fv, sol_out, outs, row, to_slot, scratch, sems, more=None):
        dbuf, fbuf, rbuf, abuf, qbuf, sbuf = scratch
        _, c = place()
        has = (c == g5) | ((c % 2 == 0) & (c // 2 != g5 // 2))
        sem = sems.at[4 + cb + pairs]
        ins = [cp.start(fv, rbuf), cp.start(inv, dbuf)]
        fs = [cp.start(fac.at[:, pl.ds(k * NB, NB)], fbuf.at[k]) for k in range(cb)]
        if more is not None:
            fs.append(cp.start(*more))

        @pl.when(has)
        def _():
            pltpu.make_async_copy(te, abuf, sem).start()

        @pl.when(jnp.logical_not(has))
        def _():
            pltpu.make_async_copy(to, abuf, sem).start()

        ins[0].wait()
        w = flip(rbuf[...])
        pltpu.make_async_copy(te, abuf, sem).wait()
        w = w - abuf[...].astype(F32)
        ins[1].wait()
        v = nn(w.astype(BF16), dbuf[...])
        wait(fs)
        multiply(qbuf, v.astype(BF16), fbuf, row)
        if more is not None:
            for d in range(pairs - 1):
                qbuf[d] = (qbuf[d].astype(F32) + more[1][d].astype(F32)).astype(BF16)
        done = [cp.start(qbuf.at[d], outs[t]) for d, t in to_slot.items()]
        sbuf[...] = jnp.transpose(v)
        wait(done + [cp.start(sbuf, sol_out)])

    solve_scratch = [(square, BF16), ((cb, NB, NB), BF16), (tall, BF16), (full, BF16), ((pairs, 2, piece, NB), BF16), (tall, F32)]

    def kernelt(*refs):
        n = len(evens5) + 1
        first, second, refs = refs[:n], refs[n : 2 * n], refs[2 * n :]
        out, abuf, bbuf, sems = refs[2], refs[-3], refs[-2], refs[-1]
        r, c = place()
        cp = Copies(sems)
        for col, x, q in zip([g5] + evens5, first, second):
            cp.branch()

            @pl.when((r == last - 2) & (c == col))
            def _(x=x, q=q):
                wait([cp.start(x, abuf), cp.start(q, bbuf)])
                abuf[...] = (abuf[...].astype(F32) + bbuf[...].astype(F32)).astype(BF16)
                cp.start(abuf, out).wait()

    n_first = 2 * len(evens5) + 2
    t5_even, y_near, sevens, tok = call(
        kernelt,
        [a3] + a4 + [a2] + q75_parts + [y_near, sevens],
        [(full, BF16), ((share, NB), BF16), (sevens.shape, BF16)],
        [(full, BF16), (full, BF16)],
        3,
        aliases={n_first: 1, n_first + 1: 2},
        order=[tok],
    )
    t5_odd = send(t5_even, within_chip(last - 2, g5))

    near_all = lax.all_gather(y_near, "col", axis=0, tiled=True)

    def kernel5(t6e, t6o, t5e, t5o, seven, fac, inv, fv, *rest):
        n = pairs + 2
        sol_out, outs = rest[n], rest[n + 1 : n + 1 + pairs]
        scratch, ebuf, sems = rest[2 * n : -2], rest[-2], rest[-1]
        r, _ = place()
        cp = Copies(sems)

        @pl.when(r == last - 1)
        def _():
            solve(cp, t6e, t6o, fac, inv, fv, sol_out, outs, last - 1, own_slots, scratch, sems)

        cp.branch()

        @pl.when(r == i)
        def _():
            solve(cp, t5e, t5o, fac, inv, fv, sol_out, outs, i, slots, scratch, sems, (seven, ebuf))

    sol, *bq, y_other, tok = call(
        kernel5,
        [t6_even, t6_odd, t5_even, t5_odd, sevens, factor, diag_inv, forward_values, sol] + bq + [y_other],
        [(tall, F32)] + [(pair_piece, BF16)] * pairs + [((share, NB), BF16)],
        solve_scratch + [((pairs - 1,) + pair_piece, BF16)],
        5 + cb + pairs,
        aliases={8 + k: k for k in range(pairs + 2)},
        order=[tok, near_all],
    )
    scattered = []
    for t in range(pairs - 1):
        to = [d for d, k in slots.items() if k == t][0]
        pairs_t = [((last - 1, b), (2 * t, b)) for b in all_cols if b * cb < last - 1]
        scattered.append(send(bq[t], pairs_t + [((i, b), (2 * to + 1, b)) for b in all_cols]))

    far_all = lax.all_gather(y_other, "col", axis=0, tiled=True)

    def load_by_parity(even, odd, buf, sem):
        r, _ = place()
        for parity, ref in enumerate((even, odd)):

            @pl.when(lax.rem(r, 2) == parity)
            def _(ref=ref):
                pltpu.make_async_copy(ref, buf, sem).start()

        return pltpu.make_async_copy(even, buf, sem)

    owners = sorted({g0, g1, g2})

    def kernelr(y0, near, far, fac, *rest):
        outs, (lbuf, abuf, pbuf, sems) = rest[:cols], rest[cols:]
        r, c = place()
        cp = Copies(sems)

        for g in owners:
            cp.branch()

            @pl.when(c == g)
            def _(g=g):
                ins = []
                if g == g0:
                    ins.append((0, cp.start(y0, abuf.at[0]), cp.start(block(fac, 0), lbuf.at[0])))
                for k, gk, even, odd in ((1, g1, far, near), (2, g2, near, far)):
                    if gk == g:
                        n = len(ins)
                        a = load_by_parity(even, odd, abuf.at[n], sems.at[4 + cols])
                        ins.append((k, a, cp.start(block(fac, k), lbuf.at[n])))
                total = None
                for n, (k, a, b) in enumerate(ins):
                    a.wait()
                    b.wait()
                    p = jnp.where(r > k, nt(abuf[n], lbuf[n]), 0.0)
                    total = p if total is None else total + p
                pbuf[...] = total.astype(BF16)
                wait(rolled(cp, pbuf, outs))

    *p_parts, tok = call(
        kernelr,
        [y0_all, near_all, far_all, factor],
        [((share, NB), BF16)] * cols,
        [((2, NB, NB), BF16), ((2,) + full, BF16), (full, BF16)],
        5 + cols,
        order=[tok],
    )
    p_got = [
        send(p_parts[s], [((a, g), (a, (g + s) % cols)) for a in range(1, rows) for g in owners]) for s in range(1, cols)
    ]

    def kernelb(own_q, *rest):
        got, (own_out, part_out, bbuf, fbuf, obuf, pbuf, sems) = rest[: pairs - 1], rest[pairs - 1 :]
        r, _ = place()
        cp = Copies(sems)
        refs = list(got) + [own_q]
        for d in range(pairs):
            cp.branch()

            @pl.when(r == 2 * d)
            def _(d=d):
                cp.start(refs[d], bbuf).wait()

            @pl.when(r == 2 * d + 1)
            def _(d=d):
                cp.start(refs[slots[d]], fbuf).wait()

        cp.branch()

        @pl.when(r == last)
        def _():
            cp.start(own_q, bbuf).wait()

        @pl.when(lax.rem(r, 2) == 0)
        def _():
            obuf[...] = bbuf[0].astype(F32)
            pbuf[...] = bbuf[1]

        @pl.when((lax.rem(r, 2) == 1) & (r < last))
        def _():
            obuf[...] = fbuf[1].astype(F32)
            pbuf[...] = fbuf[0]

        @pl.when(r == last)
        def _():
            obuf[...] = fbuf[1].astype(F32) + bbuf[1].astype(F32)
            pbuf[...] = (fbuf[0].astype(F32) + bbuf[0].astype(F32)).astype(BF16)

        cp.branch()
        wait([cp.start(pbuf, part_out), cp.start(obuf, own_out)])

    own, part, tok = call(
        kernelb,
        [bq[pairs - 1]] + scattered,
        [((piece, NB), F32), ((piece, NB), BF16)],
        [(pair_piece, BF16), (pair_piece, BF16), ((piece, NB), F32), ((piece, NB), BF16)],
        2,
        order=[tok],
    )
    theirs = send(part, all_swap)

    def kernelo(y0, near, far, rh, own_p, fs_out, side_out, abuf, tbuf, rbuf, pbuf, obuf, sems):
        _, c = place()
        cp = Copies(sems)
        ins = [cp.start(y0, abuf.at[0])]
        ins.append(load_by_parity(far, near, abuf.at[1], sems.at[7]))
        ins.append(load_by_parity(near, far, abuf.at[2], sems.at[8]))
        more = [cp.start(rh, rbuf), cp.start(own_p, pbuf)]
        done = []
        for k in range(STEPS):
            ins[k].wait()
            tbuf[k] = flip(abuf[k]).astype(BF16)
            done.append(cp.start(tbuf.at[k], fs_out.at[pl.ds(k * NB, NB)]))
        wait(more)
        side = flip(rbuf[...])
        for d in all_cols:

            @pl.when(c == d)
            def _(d=d):
                base = side[d * share : (d + 1) * share]
                obuf[...] = base - pbuf[...].astype(F32) if d in owners else base

        wait(done + [cp.start(obuf, side_out)])

    solved, side, tok = call(
        kernelo,
        [y0_all, near_all, far_all, rhs, p_parts[0]],
        [((STEPS * NB, wide), BF16), ((share, NB), F32)],
        [((STEPS,) + full, BF16), ((STEPS,) + tall, BF16), (tall, BF16), ((share, NB), BF16), ((share, NB), F32)],
        9,
        order=[tok],
    )

    rest = side - sum(x.astype(F32) for x in p_got)
    total = own + theirs.astype(F32)
    sums = jnp.concatenate([total[b * row_share : (b + 1) * row_share] for b in range(cb)], axis=1)
    return (solved, jnp.transpose(rest), jnp.transpose(sums), sol)


def solution(mesh):
    placed = (P("row", "col"), P("row", None), P("row", None), P("row", None))
    return jax.shard_map(
        local,
        mesh=mesh,
        in_specs=placed,
        out_specs=(P(), P("row", "col"), P("col", "row"), P("row", None)),
        check_vma=False,
    )
```
